768 devices in a mesh: rep: 64 (over y, x, core), row: 6 (over z_lo), col: 2 (over z_hi).
Axes of the slice: x: 4, y: 8, z: 12 (z_hi: 2, z_lo: 6; z = z_hi * 6 + z_lo), core: 2. Of those that a mesh axis runs over, the one named last changes fastest.
Arguments:
- activations: bfloat16 [49152, 2048], P(('rep', 'row'), 'col'), may hold values from -6 to 6
- out_grads: bfloat16 [49152, 2304], P(('rep', 'col'), 'row'), may hold values from -0.21875 to 0.21875
- error_buffer: float32 [131072, 2304], P(('rep', 'col'), 'row'), may hold values from -6 to 6
- right_factor: float32 [2304, 16], P('row'), may hold values from -6 to 6
Outputs:
- new_error: float32 [131072, 2304], P(('rep', 'col'), 'row')
- new_right: float32 [2304, 16], P('row')
The draws below stay inside these ranges and needn't reach their ends.
All inputs are finite; a program needn't handle non-finite values.
Results may differ from the reference program's by a relative error of at most 0.0003.
Values may be sent and summed in bfloat16 or wider, within the bound.
No kernel may reach another device: no remote copies, remote signals or barrier semaphores. Data moves between devices by JAX's collectives and lax.ppermute only.
A program may use at most 32 MiB of HBM per device.

```python
import jax
import jax.numpy as jnp
from jax import lax

DR = 2048
DC = 2304
RANK = 16
TOK_REP = 768
TOKENS = 49152
ROWS_ALL = 131072
N_REP = 64


def steps_of(key, dims, shards, low, high):
    level = 1.0
    for position, shards_of in shards:
        heights = jax.random.uniform(jax.random.fold_in(jax.random.fold_in(key, 6), position), (shards_of,), jnp.float32, low / len(shards), high / len(shards))
        level = level * jnp.repeat(jnp.exp(heights), dims[position] // shards_of).reshape((-1,) + (1,) * (len(dims) - 1 - position))
    return level


def noise(rng, dims, deviation, bound, split=(), dtype=jnp.bfloat16):
    factor_of = steps_of(rng, dims, split, -0.22, 0.18) if split else 1.0
    result = jax.random.normal(rng, dims, jnp.float32) * deviation * factor_of
    return jnp.minimum(jnp.maximum(result, -bound), bound).astype(dtype)


def setup_inputs(seed: int = 0) -> dict:
    splits = jax.random.split(jax.random.key(seed), 5)
    activations = noise(splits[0], (TOKENS, DR), 1.0, 6.0, ((0, 384), (1, 2)))
    out_grads = noise(splits[1], (TOKENS, DC), TOK_REP ** -0.5, 0.21875, ((0, 128), (1, 6)))
    error_buffer = noise(splits[2], (ROWS_ALL, DC), 1.0, 6.0, ((0, 128), (1, 6)), jnp.float32)
    right_factor = noise(splits[3], (DC, RANK), 1.0, 6.0, ((0, 6),), jnp.float32)
    return {"activations": activations, "out_grads": out_grads, "error_buffer": error_buffer, "right_factor": right_factor}


def reference(activations, out_grads, error_buffer, right_factor):
    highest = lax.Precision.HIGHEST
    acts = activations.reshape(N_REP, TOK_REP, DR)
    grads = out_grads.reshape(N_REP, TOK_REP, DC)
    errors = error_buffer.reshape(N_REP, DR, DC)

    def one_replica(items):
        act_block, grad_block, err_block = items
        product = lax.dot_general(act_block.astype(jnp.float32), grad_block.astype(jnp.float32), (((0,), (0,)), ((), ())), preferred_element_type=jnp.float32)
        return product + err_block
    target = lax.map(one_replica, (acts, grads, errors))
    left = jnp.einsum('rij,jk->ik', target, right_factor, precision=highest)
    gram = jnp.dot(left.T, left, precision=highest)
    lower = jnp.linalg.cholesky(gram)
    left_orth = jax.scipy.linalg.solve_triangular(lower, left.T, lower=True).T
    new_right = jnp.einsum('rij,ik->jk', target, left_orth, precision=highest) / N_REP
    approx = jnp.dot(left_orth, new_right.T, precision=highest)
    new_error = target - approx[None]
    return (new_error.reshape(N_REP * DR, DC), new_right)
```

```python
import jax
import jax.numpy as jnp
from jax import lax
from jax.sharding import Mesh, PartitionSpec as P

REP = ("y", "x", "core")
NEAR = ("x", "core")
HIGHEST = lax.Precision.HIGHEST


def to_all(block, axes):
    copies = jnp.broadcast_to(block, (lax.axis_size(axes), *block.shape))
    return lax.all_to_all(copies, axes, split_axis=0, concat_axis=0, tiled=True)


def summed_over(block, axes):
    return jnp.sum(to_all(block, axes), axis=0)


def split_and_summed(blocks, axes):
    return jnp.sum(lax.all_to_all(blocks, axes, split_axis=0, concat_axis=0, tiled=True), axis=0)


def dot(a, b, dims, precision=HIGHEST):
    return lax.dot_general(
        a, b, (dims, ((), ())), precision=precision, preferred_element_type=jnp.float32
    )


def body(acts, grads, err, right):
    rank = right.shape[1]
    rows, cols = err.shape
    n_row, n_col, n_near = lax.axis_size("row"), lax.axis_size("col"), lax.axis_size(NEAR)
    row, col = lax.axis_index("row"), lax.axis_index("col")
    replicas = lax.axis_size(REP)
    tokens = acts.shape[0]
    right_t = right.T

    with jax.named_scope("gather_inputs"):
        all_acts = lax.all_gather(acts, "row", axis=0, tiled=True)
        other = lax.ppermute(grads, "col", [(0, 1), (1, 0)])
        first = jnp.where(col == 0, grads, other)
        second = jnp.where(col == 0, other, grads)
        all_grads = jnp.concatenate([first, second], axis=0)

    with jax.named_scope("left_terms"):
        proj = dot(right_t, grads.astype(jnp.float32), ((1,), (1,)))
        per = n_row // n_col
        chunks = jnp.moveaxis(proj.reshape(rank, per, tokens), 1, 0)
        empty = jnp.zeros_like(chunks)
        halves = jnp.stack([jnp.where(col == i, chunks, empty) for i in range(n_col)])
        sends = jnp.broadcast_to(
            halves.reshape(n_row, 1, rank, tokens), (n_row, n_col, rank, tokens)
        ).reshape(n_row * n_col, rank, tokens)
        mine = split_and_summed(sends, ("row", "col"))
        left_t = dot(mine, acts.astype(jnp.float32), ((1,), (0,)))
        left_t = left_t + dot(right_t, err, ((1,), (1,)))

    with jax.named_scope("left_sum"):
        wide = rows // n_near
        blocks = jnp.moveaxis(left_t.reshape(rank, n_near, wide), 1, 0)
        part = split_and_summed(blocks, NEAR)
        part = summed_over(part, ("y", "row"))
        left_t = jnp.moveaxis(to_all(part, NEAR), 0, 1).reshape(rank, rows)

    with jax.named_scope("target"):
        target = dot(all_acts, all_grads, ((0,), (0,)), None) + err

    with jax.named_scope("right_sum"):
        gram = dot(left_t, left_t, ((1,), (1,))) / replicas
        right_terms = dot(left_t, target, ((1,), (0,)))
        joint = jnp.concatenate([right_terms, jnp.pad(gram, ((0, 0), (0, 128 - rank)))], axis=1)
        tiles = (cols + 128) // 128
        blocks = joint.reshape(2, rank // 2, tiles, 128).transpose(2, 0, 1, 3)
        blocks = blocks.reshape(n_near, -1, 128)
        part = split_and_summed(blocks, NEAR)
        part = summed_over(part, ("y", "col"))
        joint = to_all(part, NEAR).reshape(tiles, 2, rank // 2, 128)
        joint = joint.transpose(1, 2, 0, 3).reshape(rank, tiles * 128)
        right_t, gram = joint[:, :cols], joint[:, cols : cols + rank]

    with jax.named_scope("finish"):
        lower = jnp.linalg.cholesky(gram)
        inverse = jax.scipy.linalg.solve_triangular(
            lower, jnp.eye(rank, dtype=jnp.float32), lower=True
        )
        new_right_t = dot(inverse, right_t, ((1,), (0,))) / replicas
        orth_t = dot(inverse, left_t, ((1,), (0,)))
        new_error = target - dot(orth_t, new_right_t, ((0,), (0,)))
    return new_error, new_right_t.T


def solution(mesh):
    rep, row, col = (mesh.shape[name] for name in ("rep", "row", "col"))
    fine = Mesh(mesh.devices.reshape(rep // 8, 4, 2, row, col), ("y", "x", "core", "row", "col"))
    return jax.shard_map(
        body,
        mesh=fine,
        in_specs=(
            P((*REP, "row"), "col"),
            P((*REP, "col"), "row"),
            P((*REP, "col"), "row"),
            P("row", None),
        ),
        out_specs=(P((*REP, "col"), "row"), P("row", None)),
        check_vma=False,
    )
```

```python
import functools

import jax
import jax.numpy as jnp
from jax import lax
from jax.experimental import pallas as pl
from jax.experimental.pallas import tpu as pltpu
from jax.sharding import Mesh, PartitionSpec as P

REP = ("y", "x", "core")
NEAR = ("x", "core")
HIGHEST = lax.Precision.HIGHEST


def to_all(block, axes):
    copies = jnp.broadcast_to(block, (lax.axis_size(axes), *block.shape))
    return lax.all_to_all(copies, axes, split_axis=0, concat_axis=0, tiled=True)


def summed_over(block, axes):
    return jnp.sum(to_all(block, axes), axis=0)


def split_and_summed(blocks, axes):
    return jnp.sum(lax.all_to_all(blocks, axes, split_axis=0, concat_axis=0, tiled=True), axis=0)


def dot(a, b, dims, precision=HIGHEST):
    return lax.dot_general(
        a, b, (dims, ((), ())), precision=precision, preferred_element_type=jnp.float32
    )


def thirds(x):
    first = x.astype(jnp.bfloat16)
    rest = x - first.astype(jnp.float32)
    second = rest.astype(jnp.bfloat16)
    third = (rest - second.astype(jnp.float32)).astype(jnp.bfloat16)
    return first, second, third


def mxu(a, b, contract):
    return lax.dot_general(a, b, (contract, ((), ())), preferred_element_type=jnp.float32)


def lanes(ref, start, count):
    return jnp.concatenate([ref[start + k] for k in range(count)], axis=1)


def target_kernel(
    replicas, col_ref, acts_ref, mine_ref, other_ref, err_ref, left_ref, target_ref, joint_ref, sums
):
    step = pl.program_id(0)
    half = mine_ref.shape[0]
    mine_at = pl.multiple_of(col_ref[0] * half, half)
    other_at = pl.multiple_of((1 - col_ref[0]) * half, half)
    tile = mxu(acts_ref[pl.ds(mine_at, half), :], mine_ref[...], ((0,), (0,)))
    tile += mxu(acts_ref[pl.ds(other_at, half), :], other_ref[...], ((0,), (0,)))
    tile += err_ref[...]
    target_ref[...] = tile

    per = err_ref.shape[0] // left_ref.shape[2]
    rank = left_ref.shape[1]
    left = jnp.concatenate([left_ref[step * per + k] for k in range(per)], axis=1)
    stack = jnp.concatenate(thirds(left), axis=0)
    high, mid, low = thirds(tile)
    terms = mxu(stack, high, ((1,), (0,))) + mxu(stack, mid, ((1,), (0,)))
    right = terms[:rank] + terms[rank : 2 * rank] + terms[2 * rank :]
    right += mxu(stack[:rank], low, ((1,), (0,)))
    gram = lax.dot_general(
        left,
        left,
        (((1,), (1,)), ((), ())),
        precision=HIGHEST,
        preferred_element_type=jnp.float32,
    )
    gram = jnp.concatenate([gram, jnp.zeros((rank, 128 - rank), jnp.float32)], axis=1) / replicas
    both = jnp.concatenate([right, gram], axis=1)

    @pl.when(step == 0)
    def _():
        sums[...] = both

    @pl.when(step > 0)
    def _():
        sums[...] += both

    @pl.when(step == pl.num_programs(0) - 1)
    def _():
        for k in range(joint_ref.shape[0]):
            rows, at = (k % 2) * (rank // 2), (k // 2) * 128
            joint_ref[k] = sums[rows : rows + rank // 2, at : at + 128]


def target_and_terms(acts, mine, other, err, left, col, replicas):
    rows, cols = err.shape
    rank, wide = left.shape[1], 256
    tiles = cols // 128 + 1
    whole = lambda shape: pl.BlockSpec(shape, lambda i: (0,) * len(shape))
    return pl.pallas_call(
        functools.partial(target_kernel, replicas),
        grid=(rows // wide,),
        in_specs=[
            pl.BlockSpec(memory_space=pltpu.SMEM),
            pl.BlockSpec((acts.shape[0], wide), lambda i: (0, i)),
            whole(mine.shape),
            whole(other.shape),
            pl.BlockSpec((wide, cols), lambda i: (i, 0)),
            whole(left.shape),
        ],
        out_specs=[
            pl.BlockSpec((wide, cols), lambda i: (i, 0)),
            whole((2 * tiles, rank // 2, 128)),
        ],
        out_shape=[
            jax.ShapeDtypeStruct((rows, cols), jnp.float32),
            jax.ShapeDtypeStruct((2 * tiles, rank // 2, 128), jnp.float32),
        ],
        scratch_shapes=[pltpu.VMEM((rank, tiles * 128), jnp.float32)],
        compiler_params=pltpu.CompilerParams(vmem_limit_bytes=24 * 2**20),
    )(col.reshape(1), acts, mine, other, err, left)


def finish_kernel(replicas, joint_ref, left_ref, target_ref, error_ref, right_ref, orths, rights):
    step = pl.program_id(0)
    rank, cols = right_ref.shape

    @pl.when(step == 0)
    def _():
        halves = [
            jnp.concatenate([joint_ref[2 * c + h] for c in range(joint_ref.shape[0] // 2)], axis=1)
            for h in range(2)
        ]
        joint = jnp.concatenate(halves, axis=0)
        system = jnp.concatenate([joint, lanes(left_ref, 0, left_ref.shape[0])], axis=1)
        row_of = lax.broadcasted_iota(jnp.int32, (rank, 1), 0)
        for k in range(rank):
            column = system[:, cols + k : cols + k + 1]
            pivot = jnp.sqrt(column[k : k + 1])
            row = system[k : k + 1] / pivot
            factor = jnp.where(row_of > k, column / pivot, 0.0)
            system = jnp.where(row_of == k, row, system - factor * row)
        right = system[:, :cols] / replicas
        right_ref[...] = right
        first, second, third = thirds(right)
        rights[...] = jnp.concatenate([first, second, first, second, third, first], axis=0)
        first, second, third = thirds(system[:, cols + 128 :])
        orths[...] = jnp.concatenate([first, first, second, second, first, third], axis=0)

    wide = target_ref.shape[0]
    orth = orths[:, pl.ds(pl.multiple_of(step * wide, wide), wide)]
    error_ref[...] = target_ref[...] - mxu(orth, rights[...], ((0,), (0,)))


def finish(joint, left, target, replicas):
    rows, cols = target.shape
    rank, wide = left.shape[1], 256
    whole = lambda shape: pl.BlockSpec(shape, lambda i: (0,) * len(shape))
    return pl.pallas_call(
        functools.partial(finish_kernel, replicas),
        grid=(rows // wide,),
        in_specs=[
            whole(joint.shape),
            whole(left.shape),
            pl.BlockSpec((wide, cols), lambda i: (i, 0)),
        ],
        out_specs=[pl.BlockSpec((wide, cols), lambda i: (i, 0)), whole((rank, cols))],
        out_shape=[
            jax.ShapeDtypeStruct((rows, cols), jnp.float32),
            jax.ShapeDtypeStruct((rank, cols), jnp.float32),
        ],
        scratch_shapes=[
            pltpu.VMEM((6 * rank, rows), jnp.bfloat16),
            pltpu.VMEM((6 * rank, cols), jnp.bfloat16),
        ],
        compiler_params=pltpu.CompilerParams(vmem_limit_bytes=24 * 2**20),
    )(joint, left, target)


def body(acts, grads, err, right):
    rank = right.shape[1]
    rows = err.shape[0]
    n_row, n_col, n_near = lax.axis_size("row"), lax.axis_size("col"), lax.axis_size(NEAR)
    col = lax.axis_index("col")
    replicas = lax.axis_size(REP)
    tokens = acts.shape[0]
    right_t = right.T

    with jax.named_scope("gather_inputs"):
        all_acts = lax.all_gather(acts, "row", axis=0, tiled=True)
        other = lax.ppermute(grads, "col", [(0, 1), (1, 0)])

    with jax.named_scope("left_terms"):
        proj = dot(right_t, grads.astype(jnp.float32), ((1,), (1,)))
        per = n_row // n_col
        chunks = jnp.moveaxis(proj.reshape(rank, per, tokens), 1, 0)
        empty = jnp.zeros_like(chunks)
        halves = jnp.stack([jnp.where(col == i, chunks, empty) for i in range(n_col)])
        sends = jnp.broadcast_to(
            halves.reshape(n_row, 1, rank, tokens), (n_row, n_col, rank, tokens)
        ).reshape(n_row * n_col, rank, tokens)
        mine = split_and_summed(sends, ("row", "col"))
        left_t = dot(mine, acts.astype(jnp.float32), ((1,), (0,)))
        left_t = left_t + dot(right_t, err, ((1,), (1,)))

    with jax.named_scope("left_sum"):
        wide = rows // n_near
        blocks = jnp.moveaxis(left_t.reshape(rank, n_near, wide), 1, 0)
        part = split_and_summed(blocks, NEAR)
        part = summed_over(part, "y")
        part = summed_over(part, "row")
        left = to_all(part, NEAR)

    with jax.named_scope("target"):
        target, joint = target_and_terms(all_acts, grads, other, err, left, col, replicas)

    with jax.named_scope("right_sum"):
        part = split_and_summed(joint, NEAR)
        part = summed_over(part, ("y", "col"))
        joint = to_all(part, NEAR)

    with jax.named_scope("finish"):
        new_error, new_right_t = finish(joint, left, target, replicas)
    return new_error, new_right_t.T


def solution(mesh):
    rep, row, col = (mesh.shape[name] for name in ("rep", "row", "col"))
    fine = Mesh(mesh.devices.reshape(rep // 8, 4, 2, row, col), ("y", "x", "core", "row", "col"))
    return jax.shard_map(
        body,
        mesh=fine,
        in_specs=(
            P((*REP, "row"), "col"),
            P((*REP, "col"), "row"),
            P((*REP, "col"), "row"),
            P("row", None),
        ),
        out_specs=(P((*REP, "col"), "row"), P("row", None)),
        check_vma=False,
    )
```

```python
import functools

import jax
import jax.numpy as jnp
from jax import lax
from jax.experimental import pallas as pl
from jax.experimental.pallas import tpu as pltpu
from jax.sharding import Mesh, PartitionSpec as P

REP = ("y", "x", "core")
NEAR = ("x", "core")
HIGHEST = lax.Precision.HIGHEST


def to_all(block, axes):
    copies = jnp.broadcast_to(block, (lax.axis_size(axes), *block.shape))
    return lax.all_to_all(copies, axes, split_axis=0, concat_axis=0, tiled=True)


def summed_over(block, axes):
    return jnp.sum(to_all(block, axes), axis=0)


def split_and_summed(blocks, axes):
    return jnp.sum(lax.all_to_all(blocks, axes, split_axis=0, concat_axis=0, tiled=True), axis=0)


def dot(a, b, dims, precision=HIGHEST):
    return lax.dot_general(
        a, b, (dims, ((), ())), precision=precision, preferred_element_type=jnp.float32
    )


def thirds(x):
    first = x.astype(jnp.bfloat16)
    rest = x - first.astype(jnp.float32)
    second = rest.astype(jnp.bfloat16)
    third = (rest - second.astype(jnp.float32)).astype(jnp.bfloat16)
    return first, second, third


def mxu(a, b, contract):
    return lax.dot_general(a, b, (contract, ((), ())), preferred_element_type=jnp.float32)


def lanes(ref, start, count):
    return jnp.concatenate([ref[start + k] for k in range(count)], axis=1)


def joined(terms, rank):
    return terms[:rank] + terms[rank : 2 * rank] + terms[2 * rank :]


def projection_kernel(n_col, col_ref, right_ref, grads_ref, sends_ref):
    rank = right_ref.shape[0]
    per = sends_ref.shape[0] // n_col // n_col
    wide = sends_ref.shape[2]
    stack = jnp.concatenate(thirds(right_ref[...]), axis=0)
    proj = joined(mxu(stack, grads_ref[...], ((1,), (1,))), rank)
    for k in range(sends_ref.shape[0]):
        owner = k // n_col
        at = owner % per * wide
        keep = (col_ref[0] == owner // per).astype(jnp.float32)
        sends_ref[k] = proj[:, at : at + wide] * keep


def error_kernel(right_ref, err_ref, out_ref):
    rank = right_ref.shape[0]
    stack = jnp.concatenate(thirds(right_ref[...]), axis=0)
    wide = 256
    for k in range(err_ref.shape[0] // wide):
        high, mid, low = thirds(err_ref[k * wide : (k + 1) * wide])
        terms = joined(mxu(stack, high, ((1,), (1,))) + mxu(stack, mid, ((1,), (1,))), rank)
        out_ref[:, k * wide : (k + 1) * wide] = terms + mxu(stack[:rank], low, ((1,), (1,)))


def left_kernel(mine_ref, acts_ref, part_ref, out_ref):
    rank = mine_ref.shape[1]
    mine = mine_ref[0]
    for k in range(1, mine_ref.shape[0]):
        mine += mine_ref[k]
    stack = jnp.concatenate(thirds(mine), axis=0)
    left = joined(mxu(stack, acts_ref[...], ((1,), (0,))), rank) + part_ref[...]
    wide = out_ref.shape[2]
    for k in range(out_ref.shape[0]):
        out_ref[k] = left[:, k * wide : (k + 1) * wide]


def local_call(kernel, out_shape, *args, scalars=0):
    return pl.pallas_call(
        kernel,
        in_specs=[pl.BlockSpec(memory_space=pltpu.SMEM)] * scalars
        + [pl.BlockSpec(memory_space=pltpu.VMEM)] * (len(args) - scalars),
        out_specs=pl.BlockSpec(memory_space=pltpu.VMEM),
        out_shape=jax.ShapeDtypeStruct(out_shape, jnp.float32),
        compiler_params=pltpu.CompilerParams(vmem_limit_bytes=16 * 2**20),
    )(*args)


def target_kernel(
    replicas, col_ref, acts_ref, mine_ref, other_ref, err_ref, left_ref,
    target_ref, joint_ref, acts, other, err, target, sems, err_sems, out_sems,
):
    half = mine_ref.shape[0]
    rows = err_ref.shape[0]
    rank = left_ref.shape[1]
    wide = rows // sems.shape[0]
    mine_at = pl.multiple_of(col_ref[0] * half, half)
    other_at = pl.multiple_of((1 - col_ref[0]) * half, half)
    spans = [slice(k * wide, (k + 1) * wide) for k in range(rows // wide)]
    other_copy = pltpu.make_async_copy(other_ref, other, out_sems.at[len(spans)])
    other_copy.start()
    in_copies = []
    for k, span in enumerate(spans):
        in_copies.append(
            (
                pltpu.make_async_copy(acts_ref.at[:, span], acts.at[:, span], sems.at[k]),
                pltpu.make_async_copy(err_ref.at[span], err.at[span], err_sems.at[k]),
            )
        )
        for copy in in_copies[-1]:
            copy.start()

    left = lanes(left_ref, 0, left_ref.shape[0])
    stack = jnp.concatenate(thirds(left), axis=0)
    gram = lax.dot_general(
        left,
        left,
        (((1,), (1,)), ((), ())),
        precision=HIGHEST,
        preferred_element_type=jnp.float32,
    )
    other_copy.wait()
    sums, out_copies = None, []
    for k, span in enumerate(spans):
        for copy in in_copies[k]:
            copy.wait()
        tile = mxu(acts[pl.ds(mine_at, half), span], mine_ref[...], ((0,), (0,)))
        tile += mxu(acts[pl.ds(other_at, half), span], other[...], ((0,), (0,)))
        tile += err[span]
        target[span] = tile
        out_copies.append(pltpu.make_async_copy(target.at[span], target_ref.at[span], out_sems.at[k]))
        out_copies[-1].start()
        high, mid, low = thirds(tile)
        terms = mxu(stack[:, span], high, ((1,), (0,))) + mxu(stack[:, span], mid, ((1,), (0,)))
        right = joined(terms, rank) + mxu(stack[:rank, span], low, ((1,), (0,)))
        sums = right if sums is None else sums + right
    gram = jnp.concatenate([gram, jnp.zeros((rank, 128 - rank), jnp.float32)], axis=1) / replicas
    both = jnp.concatenate([sums, gram], axis=1)
    for k in range(joint_ref.shape[0]):
        first, at = (k % 2) * (rank // 2), (k // 2) * 128
        joint_ref[k] = both[first : first + rank // 2, at : at + 128]
    for copy in out_copies:
        copy.wait()


def target_and_terms(acts, mine, other, err, left, col, replicas):
    rows, cols = err.shape
    rank = left.shape[1]
    tiles = cols // 128 + 1
    steps = 4
    in_vmem = pl.BlockSpec(memory_space=pltpu.VMEM)
    in_hbm = pl.BlockSpec(memory_space=pltpu.HBM)
    return pl.pallas_call(
        functools.partial(target_kernel, replicas),
        in_specs=[
            pl.BlockSpec(memory_space=pltpu.SMEM),
            in_hbm,
            in_vmem,
            in_hbm,
            in_hbm,
            in_vmem,
        ],
        out_specs=[in_hbm, in_vmem],
        out_shape=[
            jax.ShapeDtypeStruct((rows, cols), jnp.float32),
            jax.ShapeDtypeStruct((2 * tiles, rank // 2, 128), jnp.float32),
        ],
        scratch_shapes=[
            pltpu.VMEM(acts.shape, acts.dtype),
            pltpu.VMEM(other.shape, other.dtype),
            pltpu.VMEM(err.shape, err.dtype),
            pltpu.VMEM(err.shape, err.dtype),
            pltpu.SemaphoreType.DMA((steps,)),
            pltpu.SemaphoreType.DMA((steps,)),
            pltpu.SemaphoreType.DMA((steps + 1,)),
        ],
        compiler_params=pltpu.CompilerParams(vmem_limit_bytes=56 * 2**20),
    )(col.reshape(1), acts, mine, other, err, left)


def finish_kernel(replicas, joint_ref, left_ref, target_ref, error_ref, right_ref, orths, rights):
    step = pl.program_id(0)
    rank, cols = right_ref.shape

    @pl.when(step == 0)
    def _():
        halves = [
            jnp.concatenate([joint_ref[2 * c + h] for c in range(joint_ref.shape[0] // 2)], axis=1)
            for h in range(2)
        ]
        joint = jnp.concatenate(halves, axis=0)
        system = jnp.concatenate([joint, lanes(left_ref, 0, left_ref.shape[0])], axis=1)
        row_of = lax.broadcasted_iota(jnp.int32, (rank, 1), 0)
        for k in range(rank - 1):
            column = system[:, cols + k : cols + k + 1]
            factor = jnp.where(row_of > k, column / column[k : k + 1], 0.0)
            system = system - factor * system[k : k + 1]
        square = system[:, cols : cols + 128]
        diagonal = lax.broadcasted_iota(jnp.int32, square.shape, 1) == row_of
        pivots = jnp.sum(jnp.where(diagonal, square, 0.0), axis=1, keepdims=True)
        system = system / jnp.sqrt(pivots)
        right = system[:, :cols] / replicas
        right_ref[...] = right
        first, second, third = thirds(right)
        rights[...] = jnp.concatenate([first, second, first, second, third, first], axis=0)
        first, second, third = thirds(system[:, cols + 128 :])
        orths[...] = jnp.concatenate([first, first, second, second, first, third], axis=0)

    wide = target_ref.shape[0]
    orth = orths[:, pl.ds(pl.multiple_of(step * wide, wide), wide)]
    error_ref[...] = target_ref[...] - mxu(orth, rights[...], ((0,), (0,)))


def finish(joint, left, target, replicas):
    rows, cols = target.shape
    rank, wide = left.shape[1], 256
    whole = lambda shape: pl.BlockSpec(shape, lambda i: (0,) * len(shape))
    return pl.pallas_call(
        functools.partial(finish_kernel, replicas),
        grid=(rows // wide,),
        in_specs=[
            whole(joint.shape),
            whole(left.shape),
            pl.BlockSpec((wide, cols), lambda i: (i, 0)),
        ],
        out_specs=[pl.BlockSpec((wide, cols), lambda i: (i, 0)), whole((rank, cols))],
        out_shape=[
            jax.ShapeDtypeStruct((rows, cols), jnp.float32),
            jax.ShapeDtypeStruct((rank, cols), jnp.float32),
        ],
        scratch_shapes=[
            pltpu.VMEM((6 * rank, rows), jnp.bfloat16),
            pltpu.VMEM((6 * rank, cols), jnp.bfloat16),
        ],
        compiler_params=pltpu.CompilerParams(vmem_limit_bytes=24 * 2**20),
    )(joint, left, target)


def body(acts, grads, err, right):
    rank = right.shape[1]
    rows = err.shape[0]
    n_row, n_col, n_near = lax.axis_size("row"), lax.axis_size("col"), lax.axis_size(NEAR)
    col = lax.axis_index("col")
    replicas = lax.axis_size(REP)
    tokens = acts.shape[0]
    right_t = right.T

    with jax.named_scope("gather_inputs"):
        all_acts = lax.all_gather(acts, "row", axis=0, tiled=True)
        other = lax.ppermute(grads, "col", [(0, 1), (1, 0)])

    with jax.named_scope("left_terms"):
        sends = local_call(
            functools.partial(projection_kernel, n_col),
            (n_row * n_col, rank, tokens),
            col.reshape(1),
            right_t,
            grads,
            scalars=1,
        )
        mine = lax.all_to_all(sends, ("row", "col"), split_axis=0, concat_axis=0, tiled=True)
        part = local_call(error_kernel, (rank, rows), right_t, err)
        blocks = local_call(left_kernel, (n_near, rank, rows // n_near), mine, acts, part)

    with jax.named_scope("left_sum"):
        part = split_and_summed(blocks, NEAR)
        part, other = lax.optimization_barrier((part, other))
        part = summed_over(part, "y")
        part = summed_over(part, "row")
        left = to_all(part, NEAR)

    with jax.named_scope("target"):
        target, joint = target_and_terms(all_acts, grads, other, err, left, col, replicas)

    with jax.named_scope("right_sum"):
        part = split_and_summed(joint, NEAR)
        part = summed_over(part, ("y", "col"))
        joint = to_all(part, NEAR)

    with jax.named_scope("finish"):
        new_error, new_right_t = finish(joint, left, target, replicas)
    return new_error, new_right_t.T


def solution(mesh):
    rep, row, col = (mesh.shape[name] for name in ("rep", "row", "col"))
    fine = Mesh(mesh.devices.reshape(rep // 8, 4, 2, row, col), ("y", "x", "core", "row", "col"))
    return jax.shard_map(
        body,
        mesh=fine,
        in_specs=(
            P((*REP, "row"), "col"),
            P((*REP, "col"), "row"),
            P((*REP, "col"), "row"),
            P("row", None),
        ),
        out_specs=(P((*REP, "col"), "row"), P("row", None)),
        check_vma=False,
    )
```

```python
import functools

import jax
import jax.numpy as jnp
from jax import lax
from jax.experimental import pallas as pl
from jax.experimental.pallas import tpu as pltpu
from jax.sharding import Mesh, PartitionSpec as P

REP = ("y", "x", "core")
NEAR = ("x", "core")
HIGHEST = lax.Precision.HIGHEST


def to_all(block, axes):
    copies = jnp.broadcast_to(block, (lax.axis_size(axes), *block.shape))
    return lax.all_to_all(copies, axes, split_axis=0, concat_axis=0, tiled=True)


def summed_over(block, axes):
    return jnp.sum(to_all(block, axes), axis=0)


def split_and_summed(blocks, axes):
    return jnp.sum(lax.all_to_all(blocks, axes, split_axis=0, concat_axis=0, tiled=True), axis=0)


def dot(a, b, dims, precision=HIGHEST):
    return lax.dot_general(
        a, b, (dims, ((), ())), precision=precision, preferred_element_type=jnp.float32
    )


def thirds(x):
    first = x.astype(jnp.bfloat16)
    rest = x - first.astype(jnp.float32)
    second = rest.astype(jnp.bfloat16)
    third = (rest - second.astype(jnp.float32)).astype(jnp.bfloat16)
    return first, second, third


def mxu(a, b, contract):
    return lax.dot_general(a, b, (contract, ((), ())), preferred_element_type=jnp.float32)


def lanes(ref, start, count):
    return jnp.concatenate([ref[start + k] for k in range(count)], axis=1)


def joined(terms, rank):
    return terms[:rank] + terms[rank : 2 * rank] + terms[2 * rank :]


def projection_kernel(n_col, col_ref, right_ref, grads_ref, sends_ref):
    rank = right_ref.shape[0]
    per = sends_ref.shape[0] // n_col // n_col
    wide = sends_ref.shape[2]
    stack = jnp.concatenate(thirds(right_ref[...]), axis=0)
    proj = joined(mxu(stack, grads_ref[...], ((1,), (1,))), rank)
    for k in range(sends_ref.shape[0]):
        owner = k // n_col
        at = owner % per * wide
        keep = (col_ref[0] == owner // per).astype(jnp.float32)
        sends_ref[k] = proj[:, at : at + wide] * keep


def error_kernel(right_ref, err_ref, out_ref):
    rank = right_ref.shape[0]
    stack = jnp.concatenate(thirds(right_ref[...]), axis=0)
    wide = 256
    for k in range(err_ref.shape[0] // wide):
        high, mid, low = thirds(err_ref[k * wide : (k + 1) * wide])
        terms = joined(mxu(stack, high, ((1,), (1,))) + mxu(stack, mid, ((1,), (1,))), rank)
        out_ref[:, k * wide : (k + 1) * wide] = terms + mxu(stack[:rank], low, ((1,), (1,)))


def left_kernel(mine_ref, acts_ref, part_ref, out_ref):
    rank = mine_ref.shape[1]
    mine = mine_ref[0]
    for k in range(1, mine_ref.shape[0]):
        mine += mine_ref[k]
    stack = jnp.concatenate(thirds(mine), axis=0)
    left = joined(mxu(stack, acts_ref[...], ((1,), (0,))), rank) + part_ref[...]
    wide = out_ref.shape[2]
    for k in range(out_ref.shape[0]):
        out_ref[k] = left[:, k * wide : (k + 1) * wide]


def local_call(kernel, out_shape, *args, scalars=0, limit=16):
    return pl.pallas_call(
        kernel,
        in_specs=[pl.BlockSpec(memory_space=pltpu.SMEM)] * scalars
        + [pl.BlockSpec(memory_space=pltpu.VMEM)] * (len(args) - scalars),
        out_specs=pl.BlockSpec(memory_space=pltpu.VMEM),
        out_shape=jax.ShapeDtypeStruct(out_shape, jnp.float32),
        compiler_params=pltpu.CompilerParams(vmem_limit_bytes=limit * 2**20),
    )(*args)


def target_kernel(replicas, n_acts, col_ref, *refs):
    acts_refs, refs = refs[:n_acts], refs[n_acts:]
    mine_ref, other_ref, err_ref, left_ref, target_ref, joint_ref = refs
    half = mine_ref.shape[0]
    rank = left_ref.shape[1]
    wide = 256
    mine_at = pl.multiple_of(col_ref[0] * half, half)
    other_at = pl.multiple_of((1 - col_ref[0]) * half, half)
    left = lanes(left_ref, 0, left_ref.shape[0])
    stack = jnp.concatenate(thirds(left), axis=0)
    gram = lax.dot_general(
        left,
        left,
        (((1,), (1,)), ((), ())),
        precision=HIGHEST,
        preferred_element_type=jnp.float32,
    )
    sums = None
    for k in range(err_ref.shape[0] // wide):
        span = slice(k * wide, (k + 1) * wide)
        acts_ref = acts_refs[k * wide // acts_refs[0].shape[1]]
        at = k * wide % acts_ref.shape[1]
        tile = mxu(acts_ref[pl.ds(mine_at, half), at : at + wide], mine_ref[...], ((0,), (0,)))
        tile += mxu(acts_ref[pl.ds(other_at, half), at : at + wide], other_ref[...], ((0,), (0,)))
        tile += err_ref[span]
        target_ref[span] = tile
        high, mid, low = thirds(tile)
        terms = mxu(stack[:, span], high, ((1,), (0,))) + mxu(stack[:, span], mid, ((1,), (0,)))
        right = joined(terms, rank) + mxu(stack[:rank, span], low, ((1,), (0,)))
        sums = right if sums is None else sums + right
    gram = jnp.concatenate([gram, jnp.zeros((rank, 128 - rank), jnp.float32)], axis=1) / replicas
    both = jnp.concatenate([sums, gram], axis=1)
    for k in range(joint_ref.shape[0]):
        first, at = (k % 2) * (rank // 2), (k // 2) * 128
        joint_ref[k] = both[first : first + rank // 2, at : at + 128]


def target_and_terms(acts, mine, other, err, left, col, replicas):
    rows, cols = err.shape
    rank = left.shape[1]
    tiles = cols // 128 + 1
    in_vmem = pl.BlockSpec(memory_space=pltpu.VMEM)
    return pl.pallas_call(
        functools.partial(target_kernel, replicas, len(acts)),
        in_specs=[pl.BlockSpec(memory_space=pltpu.SMEM)] + [in_vmem] * (4 + len(acts)),
        out_specs=[in_vmem, in_vmem],
        out_shape=[
            jax.ShapeDtypeStruct((rows, cols), jnp.float32),
            jax.ShapeDtypeStruct((2 * tiles, rank // 2, 128), jnp.float32),
        ],
        compiler_params=pltpu.CompilerParams(vmem_limit_bytes=24 * 2**20),
    )(col.reshape(1), *acts, mine, other, err, left)


def finish_kernel(replicas, joint_ref, left_ref, target_ref, error_ref, right_ref, error, sems):
    rank, cols = right_ref.shape
    halves = [
        jnp.concatenate([joint_ref[2 * c + h] for c in range(joint_ref.shape[0] // 2)], axis=1)
        for h in range(2)
    ]
    joint = jnp.concatenate(halves, axis=0)
    system = jnp.concatenate([joint, lanes(left_ref, 0, left_ref.shape[0])], axis=1)
    row_of = lax.broadcasted_iota(jnp.int32, (rank, 1), 0)
    for k in range(rank - 1):
        column = system[:, cols + k : cols + k + 1]
        factor = jnp.where(row_of > k, column / column[k : k + 1], 0.0)
        system = system - factor * system[k : k + 1]
    square = system[:, cols : cols + 128]
    diagonal = lax.broadcasted_iota(jnp.int32, square.shape, 1) == row_of
    pivots = jnp.sum(jnp.where(diagonal, square, 0.0), axis=1, keepdims=True)
    system = system / jnp.sqrt(pivots)
    right = system[:, :cols] / replicas
    right_ref[...] = right
    first, second, third = thirds(right)
    rights = jnp.concatenate([first, second, first, second, third, first], axis=0)
    first, second, third = thirds(system[:, cols + 128 :])
    orths = jnp.concatenate([first, first, second, second, first, third], axis=0)
    wide = target_ref.shape[0] // sems.shape[0]
    copies = []
    for k in range(sems.shape[0]):
        span = slice(k * wide, (k + 1) * wide)
        error[span] = target_ref[span] - mxu(orths[:, span], rights, ((0,), (0,)))
        copies.append(pltpu.make_async_copy(error.at[span], error_ref.at[span], sems.at[k]))
        copies[-1].start()
    for copy in copies:
        copy.wait()


def finish(joint, left, target, replicas):
    rows, cols = target.shape
    rank = left.shape[1]
    in_vmem = pl.BlockSpec(memory_space=pltpu.VMEM)
    return pl.pallas_call(
        functools.partial(finish_kernel, replicas),
        in_specs=[in_vmem] * 3,
        out_specs=[pl.BlockSpec(memory_space=pl.ANY), in_vmem],
        out_shape=[
            jax.ShapeDtypeStruct((rows, cols), jnp.float32),
            jax.ShapeDtypeStruct((rank, cols), jnp.float32),
        ],
        scratch_shapes=[
            pltpu.VMEM((rows, cols), jnp.float32),
            pltpu.SemaphoreType.DMA((4,)),
        ],
        compiler_params=pltpu.CompilerParams(vmem_limit_bytes=24 * 2**20),
    )(joint, left, target)


def body(acts, grads, err, right):
    rank = right.shape[1]
    rows = err.shape[0]
    n_row, n_col, n_near = lax.axis_size("row"), lax.axis_size("col"), lax.axis_size(NEAR)
    col = lax.axis_index("col")
    replicas = lax.axis_size(REP)
    tokens = acts.shape[0]
    right_t = right.T

    with jax.named_scope("gather_inputs"):
        all_acts = [lax.all_gather(acts, "row", axis=0, tiled=True)]
        other = lax.ppermute(grads, "col", [(0, 1), (1, 0)])

    with jax.named_scope("left_terms"):
        sends = local_call(
            functools.partial(projection_kernel, n_col),
            (n_row * n_col, rank, tokens),
            col.reshape(1),
            right_t,
            grads,
            scalars=1,
            limit=56,
        )
        mine = lax.all_to_all(sends, ("row", "col"), split_axis=0, concat_axis=0, tiled=True)
        part = local_call(error_kernel, (rank, rows), right_t, err, limit=56)
        blocks = local_call(left_kernel, (n_near, rank, rows // n_near), mine, acts, part)

    with jax.named_scope("left_sum"):
        part = split_and_summed(blocks, NEAR)
        part = summed_over(part, "y")
        part = summed_over(part, "row")
        part, other = lax.optimization_barrier((part, other))
        left = to_all(part, NEAR)

    with jax.named_scope("target"):
        target, joint = target_and_terms(all_acts, grads, other, err, left, col, replicas)

    with jax.named_scope("right_sum"):
        part = split_and_summed(joint, NEAR)
        part = summed_over(part, ("y", "col"))
        joint = to_all(part, NEAR)

    with jax.named_scope("finish"):
        new_error, new_right_t = finish(joint, left, target, replicas)
    return new_error, new_right_t.T


def solution(mesh):
    rep, row, col = (mesh.shape[name] for name in ("rep", "row", "col"))
    fine = Mesh(mesh.devices.reshape(rep // 8, 4, 2, row, col), ("y", "x", "core", "row", "col"))
    return jax.shard_map(
        body,
        mesh=fine,
        in_specs=(
            P((*REP, "row"), "col"),
            P((*REP, "col"), "row"),
            P((*REP, "col"), "row"),
            P("row", None),
        ),
        out_specs=(P((*REP, "col"), "row"), P("row", None)),
        check_vma=False,
    )
```

```python
import functools

import jax
import jax.numpy as jnp
from jax import lax
from jax.experimental import pallas as pl
from jax.experimental.pallas import tpu as pltpu
from jax.sharding import Mesh, PartitionSpec as P

REP = ("y", "x", "core")
NEAR = ("x", "core")
HIGHEST = lax.Precision.HIGHEST


def to_all(block, axes):
    copies = jnp.broadcast_to(block, (lax.axis_size(axes), *block.shape))
    return lax.all_to_all(copies, axes, split_axis=0, concat_axis=0, tiled=True)


def summed_over(block, axes):
    return jnp.sum(to_all(block, axes), axis=0)


def split_and_summed(blocks, axes):
    return jnp.sum(lax.all_to_all(blocks, axes, split_axis=0, concat_axis=0, tiled=True), axis=0)


def dot(a, b, dims, precision=HIGHEST):
    return lax.dot_general(
        a, b, (dims, ((), ())), precision=precision, preferred_element_type=jnp.float32
    )


def thirds(x):
    first = x.astype(jnp.bfloat16)
    rest = x - first.astype(jnp.float32)
    second = rest.astype(jnp.bfloat16)
    third = (rest - second.astype(jnp.float32)).astype(jnp.bfloat16)
    return first, second, third


def mxu(a, b, contract):
    return lax.dot_general(a, b, (contract, ((), ())), preferred_element_type=jnp.float32)


def lanes(ref, start, count):
    return jnp.concatenate([ref[start + k] for k in range(count)], axis=1)


def joined(terms, rank):
    return terms[:rank] + terms[rank : 2 * rank] + terms[2 * rank :]


def projection_kernel(n_col, col_ref, right_ref, grads_ref, sends_ref):
    rank = right_ref.shape[0]
    per = sends_ref.shape[0] // n_col // n_col
    wide = sends_ref.shape[2]
    stack = jnp.concatenate(thirds(right_ref[...]), axis=0)
    proj = joined(mxu(stack, grads_ref[...], ((1,), (1,))), rank)
    for k in range(sends_ref.shape[0]):
        owner = k // n_col
        at = owner % per * wide
        keep = (col_ref[0] == owner // per).astype(jnp.float32)
        sends_ref[k] = proj[:, at : at + wide] * keep


def error_kernel(right_ref, err_ref, out_ref):
    rank = right_ref.shape[0]
    stack = jnp.concatenate(thirds(right_ref[...]), axis=0)
    wide = 256
    for k in range(err_ref.shape[0] // wide):
        high, mid, low = thirds(err_ref[k * wide : (k + 1) * wide])
        terms = joined(mxu(stack, high, ((1,), (1,))) + mxu(stack, mid, ((1,), (1,))), rank)
        out_ref[:, k * wide : (k + 1) * wide] = terms + mxu(stack[:rank], low, ((1,), (1,)))


def left_kernel(mine_ref, acts_ref, part_ref, out_ref):
    rank = mine_ref.shape[1]
    mine = mine_ref[0]
    for k in range(1, mine_ref.shape[0]):
        mine += mine_ref[k]
    stack = jnp.concatenate(thirds(mine), axis=0)
    left = joined(mxu(stack, acts_ref[...], ((1,), (0,))), rank) + part_ref[...]
    wide = out_ref.shape[2]
    for k in range(out_ref.shape[0]):
        out_ref[k] = left[:, k * wide : (k + 1) * wide]


def local_call(kernel, out_shape, *args, scalars=0, limit=16):
    return pl.pallas_call(
        kernel,
        in_specs=[pl.BlockSpec(memory_space=pltpu.SMEM)] * scalars
        + [pl.BlockSpec(memory_space=pltpu.VMEM)] * (len(args) - scalars),
        out_specs=pl.BlockSpec(memory_space=pltpu.VMEM),
        out_shape=jax.ShapeDtypeStruct(out_shape, jnp.float32),
        compiler_params=pltpu.CompilerParams(vmem_limit_bytes=limit * 2**20),
    )(*args)


def target_kernel(
    replicas, order, col_ref, acts_ref, mine_ref, other_ref, err_ref, left_ref,
    target_ref, joint_ref, grads,
):
    rank = left_ref.shape[1]
    wide = 256
    half = mine_ref.shape[0]
    per = len(order) // 2
    chunk = half // per
    for k, place in enumerate(order):
        source = slice(place % per * chunk, place % per * chunk + chunk)
        is_mine = col_ref[0] == place // per
        grads[k * chunk : (k + 1) * chunk] = jnp.where(is_mine, mine_ref[source], other_ref[source])
    left = lanes(left_ref, 0, left_ref.shape[0])
    stack = jnp.concatenate(thirds(left), axis=0)
    gram = lax.dot_general(
        left,
        left,
        (((1,), (1,)), ((), ())),
        precision=HIGHEST,
        preferred_element_type=jnp.float32,
    )
    sums = None
    for k in range(err_ref.shape[0] // wide):
        span = slice(k * wide, (k + 1) * wide)
        tile = mxu(acts_ref[:, span], grads[...], ((0,), (0,))) + err_ref[span]
        target_ref[span] = tile
        high, mid, low = thirds(tile)
        terms = mxu(stack[:, span], high, ((1,), (0,))) + mxu(stack[:, span], mid, ((1,), (0,)))
        right = joined(terms, rank) + mxu(stack[:rank, span], low, ((1,), (0,)))
        sums = right if sums is None else sums + right
    gram = jnp.concatenate([gram, jnp.zeros((rank, 128 - rank), jnp.float32)], axis=1) / replicas
    both = jnp.concatenate([sums, gram], axis=1)
    for k in range(joint_ref.shape[0]):
        first, at = (k % 2) * (rank // 2), (k // 2) * 128
        joint_ref[k] = both[first : first + rank // 2, at : at + 128]


def target_and_terms(acts, mine, other, err, left, col, replicas, order):
    rows, cols = err.shape
    rank = left.shape[1]
    tiles = cols // 128 + 1
    in_vmem = pl.BlockSpec(memory_space=pltpu.VMEM)
    return pl.pallas_call(
        functools.partial(target_kernel, replicas, order),
        in_specs=[pl.BlockSpec(memory_space=pltpu.SMEM)] + [in_vmem] * 5,
        out_specs=[in_vmem, in_vmem],
        out_shape=[
            jax.ShapeDtypeStruct((rows, cols), jnp.float32),
            jax.ShapeDtypeStruct((2 * tiles, rank // 2, 128), jnp.float32),
        ],
        scratch_shapes=[pltpu.VMEM((2 * mine.shape[0], cols), mine.dtype)],
        compiler_params=pltpu.CompilerParams(vmem_limit_bytes=24 * 2**20),
    )(col.reshape(1), acts, mine, other, err, left)


def finish_kernel(replicas, joint_ref, left_ref, target_ref, error_ref, right_ref, error, sems):
    rank, cols = right_ref.shape
    halves = [
        jnp.concatenate([joint_ref[2 * c + h] for c in range(joint_ref.shape[0] // 2)], axis=1)
        for h in range(2)
    ]
    joint = jnp.concatenate(halves, axis=0)
    system = jnp.concatenate([joint, lanes(left_ref, 0, left_ref.shape[0])], axis=1)
    row_of = lax.broadcasted_iota(jnp.int32, (rank, 1), 0)
    for k in range(rank - 1):
        column = system[:, cols + k : cols + k + 1]
        factor = jnp.where(row_of > k, column / column[k : k + 1], 0.0)
        system = system - factor * system[k : k + 1]
    square = system[:, cols : cols + 128]
    diagonal = lax.broadcasted_iota(jnp.int32, square.shape, 1) == row_of
    pivots = jnp.sum(jnp.where(diagonal, square, 0.0), axis=1, keepdims=True)
    system = system / jnp.sqrt(pivots)
    right = system[:, :cols] / replicas
    right_ref[...] = right
    first, second, third = thirds(right)
    rights = jnp.concatenate([first, second, first, second, third, first], axis=0)
    first, second, third = thirds(system[:, cols + 128 :])
    orths = jnp.concatenate([first, first, second, second, first, third], axis=0)
    wide = target_ref.shape[0] // sems.shape[0]
    copies = []
    for k in range(sems.shape[0]):
        span = slice(k * wide, (k + 1) * wide)
        error[span] = target_ref[span] - mxu(orths[:, span], rights, ((0,), (0,)))
        copies.append(pltpu.make_async_copy(error.at[span], error_ref.at[span], sems.at[k]))
        copies[-1].start()
    for copy in copies:
        copy.wait()


def finish(joint, left, target, replicas):
    rows, cols = target.shape
    rank = left.shape[1]
    in_vmem = pl.BlockSpec(memory_space=pltpu.VMEM)
    return pl.pallas_call(
        functools.partial(finish_kernel, replicas),
        in_specs=[in_vmem] * 3,
        out_specs=[pl.BlockSpec(memory_space=pl.ANY), in_vmem],
        out_shape=[
            jax.ShapeDtypeStruct((rows, cols), jnp.float32),
            jax.ShapeDtypeStruct((rank, cols), jnp.float32),
        ],
        scratch_shapes=[
            pltpu.VMEM((rows, cols), jnp.float32),
            pltpu.SemaphoreType.DMA((4,)),
        ],
        compiler_params=pltpu.CompilerParams(vmem_limit_bytes=24 * 2**20),
    )(joint, left, target)


def body(acts, grads, err, right):
    rank = right.shape[1]
    rows = err.shape[0]
    n_row, n_col, n_near = lax.axis_size("row"), lax.axis_size("col"), lax.axis_size(NEAR)
    col = lax.axis_index("col")
    replicas = lax.axis_size(REP)
    tokens = acts.shape[0]
    right_t = right.T

    with jax.named_scope("gather_inputs"):
        order = [*range(0, n_row, 2), *reversed(range(1, n_row, 2))]
        all_acts = lax.all_gather(acts, "row", axis=0, tiled=True, axis_index_groups=[order])
        other = lax.ppermute(grads, "col", [(0, 1), (1, 0)])

    with jax.named_scope("left_terms"):
        sends = local_call(
            functools.partial(projection_kernel, n_col),
            (n_row * n_col, rank, tokens),
            col.reshape(1),
            right_t,
            grads,
            scalars=1,
            limit=56,
        )
        mine = lax.all_to_all(sends, ("row", "col"), split_axis=0, concat_axis=0, tiled=True)
        part = local_call(error_kernel, (rank, rows), right_t, err, limit=56)
        blocks = local_call(left_kernel, (n_near, rank, rows // n_near), mine, acts, part)

    with jax.named_scope("left_sum"):
        part = split_and_summed(blocks, NEAR)
        part = summed_over(part, "y")
        part = summed_over(part, "row")
        part, other = lax.optimization_barrier((part, other))
        left = to_all(part, NEAR)

    with jax.named_scope("target"):
        target, joint = target_and_terms(
            all_acts, grads, other, err, left, col, replicas, order
        )

    with jax.named_scope("right_sum"):
        part = split_and_summed(joint, NEAR)
        part = summed_over(part, ("y", "col"))
        joint = to_all(part, NEAR)

    with jax.named_scope("finish"):
        new_error, new_right_t = finish(joint, left, target, replicas)
    return new_error, new_right_t.T


def solution(mesh):
    rep, row, col = (mesh.shape[name] for name in ("rep", "row", "col"))
    fine = Mesh(mesh.devices.reshape(rep // 8, 4, 2, row, col), ("y", "x", "core", "row", "col"))
    return jax.shard_map(
        body,
        mesh=fine,
        in_specs=(
            P((*REP, "row"), "col"),
            P((*REP, "col"), "row"),
            P((*REP, "col"), "row"),
            P("row", None),
        ),
        out_specs=(P((*REP, "col"), "row"), P("row", None)),
        check_vma=False,
    )
```

```python
import functools

import jax
import jax.numpy as jnp
from jax import lax
from jax.experimental import pallas as pl
from jax.experimental.pallas import tpu as pltpu
from jax.sharding import Mesh, PartitionSpec as P

REP = ("y", "x", "core")
NEAR = ("x", "core")
ROW = ("far", "next")
HIGHEST = lax.Precision.HIGHEST


def to_all(block, axes):
    copies = jnp.broadcast_to(block, (lax.axis_size(axes), *block.shape))
    return lax.all_to_all(copies, axes, split_axis=0, concat_axis=0, tiled=True)


def summed_over(block, axes):
    return jnp.sum(to_all(block, axes), axis=0)


def split_and_summed(blocks, axes):
    return jnp.sum(lax.all_to_all(blocks, axes, split_axis=0, concat_axis=0, tiled=True), axis=0)


def dot(a, b, dims, precision=HIGHEST):
    return lax.dot_general(
        a, b, (dims, ((), ())), precision=precision, preferred_element_type=jnp.float32
    )


def thirds(x):
    first = x.astype(jnp.bfloat16)
    rest = x - first.astype(jnp.float32)
    second = rest.astype(jnp.bfloat16)
    third = (rest - second.astype(jnp.float32)).astype(jnp.bfloat16)
    return first, second, third


def mxu(a, b, contract):
    return lax.dot_general(a, b, (contract, ((), ())), preferred_element_type=jnp.float32)


def lanes(ref, start, count):
    return jnp.concatenate([ref[start + k] for k in range(count)], axis=1)


def joined(terms, rank):
    return terms[:rank] + terms[rank : 2 * rank] + terms[2 * rank :]


def projection_kernel(n_col, col_ref, right_ref, grads_ref, sends_ref):
    rank = right_ref.shape[0]
    per = sends_ref.shape[0] // n_col // n_col
    wide = sends_ref.shape[2]
    stack = jnp.concatenate(thirds(right_ref[...]), axis=0)
    proj = joined(mxu(stack, grads_ref[...], ((1,), (1,))), rank)
    for k in range(sends_ref.shape[0]):
        owner = k // n_col
        at = owner % per * wide
        keep = (col_ref[0] == owner // per).astype(jnp.float32)
        sends_ref[k] = proj[:, at : at + wide] * keep


def error_kernel(right_ref, err_ref, out_ref):
    rank = right_ref.shape[0]
    stack = jnp.concatenate(thirds(right_ref[...]), axis=0)
    wide = 256
    for k in range(err_ref.shape[0] // wide):
        high, mid, low = thirds(err_ref[k * wide : (k + 1) * wide])
        terms = joined(mxu(stack, high, ((1,), (1,))) + mxu(stack, mid, ((1,), (1,))), rank)
        out_ref[:, k * wide : (k + 1) * wide] = terms + mxu(stack[:rank], low, ((1,), (1,)))


def left_kernel(mine_ref, acts_ref, part_ref, out_ref):
    rank = mine_ref.shape[1]
    mine = mine_ref[0]
    for k in range(1, mine_ref.shape[0]):
        mine += mine_ref[k]
    stack = jnp.concatenate(thirds(mine), axis=0)
    left = joined(mxu(stack, acts_ref[...], ((1,), (0,))), rank) + part_ref[...]
    wide = out_ref.shape[2]
    for k in range(out_ref.shape[0]):
        out_ref[k] = left[:, k * wide : (k + 1) * wide]


def local_call(kernel, out_shape, *args, scalars=0, limit=16):
    return pl.pallas_call(
        kernel,
        in_specs=[pl.BlockSpec(memory_space=pltpu.SMEM)] * scalars
        + [pl.BlockSpec(memory_space=pltpu.VMEM)] * (len(args) - scalars),
        out_specs=pl.BlockSpec(memory_space=pltpu.VMEM),
        out_shape=jax.ShapeDtypeStruct(out_shape, jnp.float32),
        compiler_params=pltpu.CompilerParams(vmem_limit_bytes=limit * 2**20),
    )(*args)


def target_kernel(
    replicas, chunk, same_ref, acts_ref, mine_ref, other_ref, err_ref, left_ref,
    target_ref, joint_ref, grads,
):
    rank = left_ref.shape[1]
    wide = 256
    same = same_ref[0] == 1
    for k in range(mine_ref.shape[0] // chunk):
        source = slice(k * chunk, (k + 1) * chunk)
        mine, other = mine_ref[source], other_ref[source]
        grads[2 * k * chunk : (2 * k + 1) * chunk] = jnp.where(same, mine, other)
        grads[(2 * k + 1) * chunk : (2 * k + 2) * chunk] = jnp.where(same, other, mine)
    left = lanes(left_ref, 0, left_ref.shape[0])
    stack = jnp.concatenate(thirds(left), axis=0)
    gram = lax.dot_general(
        left,
        left,
        (((1,), (1,)), ((), ())),
        precision=HIGHEST,
        preferred_element_type=jnp.float32,
    )
    sums = None
    for k in range(err_ref.shape[0] // wide):
        span = slice(k * wide, (k + 1) * wide)
        tile = mxu(acts_ref[:, span], grads[...], ((0,), (0,))) + err_ref[span]
        target_ref[span] = tile
        high, mid, low = thirds(tile)
        terms = mxu(stack[:, span], high, ((1,), (0,))) + mxu(stack[:, span], mid, ((1,), (0,)))
        right = joined(terms, rank) + mxu(stack[:rank, span], low, ((1,), (0,)))
        sums = right if sums is None else sums + right
    gram = jnp.concatenate([gram, jnp.zeros((rank, 128 - rank), jnp.float32)], axis=1) / replicas
    both = jnp.concatenate([sums, gram], axis=1)
    for k in range(joint_ref.shape[0]):
        first, at = (k % 2) * (rank // 2), (k // 2) * 128
        joint_ref[k] = both[first : first + rank // 2, at : at + 128]


def target_and_terms(acts, mine, other, err, left, same, replicas, chunk):
    rows, cols = err.shape
    rank = left.shape[1]
    tiles = cols // 128 + 1
    in_vmem = pl.BlockSpec(memory_space=pltpu.VMEM)
    return pl.pallas_call(
        functools.partial(target_kernel, replicas, chunk),
        in_specs=[pl.BlockSpec(memory_space=pltpu.SMEM)] + [in_vmem] * 5,
        out_specs=[in_vmem, in_vmem],
        out_shape=[
            jax.ShapeDtypeStruct((rows, cols), jnp.float32),
            jax.ShapeDtypeStruct((2 * tiles, rank // 2, 128), jnp.float32),
        ],
        scratch_shapes=[pltpu.VMEM((2 * mine.shape[0], cols), mine.dtype)],
        compiler_params=pltpu.CompilerParams(vmem_limit_bytes=16 * 2**20),
    )(same.astype(jnp.int32).reshape(1), acts, mine, other, err, left)


def finish_kernel(replicas, joint_ref, left_ref, target_ref, error_ref, right_ref, error, sems):
    rank, cols = right_ref.shape
    halves = [
        jnp.concatenate([joint_ref[2 * c + h] for c in range(joint_ref.shape[0] // 2)], axis=1)
        for h in range(2)
    ]
    joint = jnp.concatenate(halves, axis=0)
    system = jnp.concatenate([joint, lanes(left_ref, 0, left_ref.shape[0])], axis=1)
    row_of = lax.broadcasted_iota(jnp.int32, (rank, 1), 0)
    for k in range(rank - 1):
        column = system[:, cols + k : cols + k + 1]
        factor = jnp.where(row_of > k, column / column[k : k + 1], 0.0)
        system = system - factor * system[k : k + 1]
    square = system[:, cols : cols + 128]
    diagonal = lax.broadcasted_iota(jnp.int32, square.shape, 1) == row_of
    pivots = jnp.sum(jnp.where(diagonal, square, 0.0), axis=1, keepdims=True)
    system = system / jnp.sqrt(pivots)
    right = system[:, :cols] / replicas
    right_ref[...] = right
    first, second, third = thirds(right)
    rights = jnp.concatenate([first, second, first, second, third, first], axis=0)
    first, second, third = thirds(system[:, cols + 128 :])
    orths = jnp.concatenate([first, first, second, second, first, third], axis=0)
    wide = target_ref.shape[0] // sems.shape[0]
    copies = []
    for k in range(sems.shape[0]):
        span = slice(k * wide, (k + 1) * wide)
        error[span] = target_ref[span] - mxu(orths[:, span], rights, ((0,), (0,)))
        copies.append(pltpu.make_async_copy(error.at[span], error_ref.at[span], sems.at[k]))
        copies[-1].start()
    for copy in copies:
        copy.wait()


def finish(joint, left, target, replicas):
    rows, cols = target.shape
    rank = left.shape[1]
    in_vmem = pl.BlockSpec(memory_space=pltpu.VMEM)
    return pl.pallas_call(
        functools.partial(finish_kernel, replicas),
        in_specs=[in_vmem] * 3,
        out_specs=[pl.BlockSpec(memory_space=pl.ANY), in_vmem],
        out_shape=[
            jax.ShapeDtypeStruct((rows, cols), jnp.float32),
            jax.ShapeDtypeStruct((rank, cols), jnp.float32),
        ],
        scratch_shapes=[
            pltpu.VMEM((rows, cols), jnp.float32),
            pltpu.SemaphoreType.DMA((4,)),
        ],
        compiler_params=pltpu.CompilerParams(vmem_limit_bytes=16 * 2**20),
    )(joint, left, target)


def body(acts, grads, err, right):
    rank = right.shape[1]
    rows = err.shape[0]
    n_row, n_col, n_near = lax.axis_size(ROW), lax.axis_size("col"), lax.axis_size(NEAR)
    col = lax.axis_index("col")
    replicas = lax.axis_size(REP)
    tokens = acts.shape[0]
    right_t = right.T

    with jax.named_scope("gather_inputs"):
        swapped = lax.ppermute(acts, "far", [(0, 1), (1, 0)])
        pair = jnp.concatenate([acts, swapped], axis=0)
        other = lax.ppermute(grads, "col", [(0, 1), (1, 0)])

    with jax.named_scope("left_terms"):
        sends = local_call(
            functools.partial(projection_kernel, n_col),
            (n_row * n_col, rank, tokens),
            col.reshape(1),
            right_t,
            grads,
            scalars=1,
            limit=56,
        )
        mine = lax.all_to_all(sends, (*ROW, "col"), split_axis=0, concat_axis=0, tiled=True)
        part = local_call(error_kernel, (rank, rows), right_t, err)
        blocks = local_call(left_kernel, (n_near, rank, rows // n_near), mine, acts, part)

    with jax.named_scope("left_sum"):
        blocks, pair = lax.optimization_barrier((blocks, pair))
        all_acts = lax.all_gather(pair, "next", axis=0, tiled=True)
        part = split_and_summed(blocks, NEAR)
        part = summed_over(part, "y")
        part = summed_over(part, ROW)
        part, other = lax.optimization_barrier((part, other))
        left = to_all(part, NEAR)

    with jax.named_scope("target"):
        target, joint = target_and_terms(
            all_acts, grads, other, err, left, col == lax.axis_index("far"), replicas, tokens
        )

    with jax.named_scope("right_sum"):
        part = split_and_summed(joint, NEAR)
        part = summed_over(part, ("y", "col"))
        joint = to_all(part, NEAR)

    with jax.named_scope("finish"):
        new_error, new_right_t = finish(joint, left, target, replicas)
    return new_error, new_right_t.T


def solution(mesh):
    rep, row, col = (mesh.shape[name] for name in ("rep", "row", "col"))
    fine = Mesh(
        mesh.devices.reshape(rep // 8, 4, 2, 2, row // 2, col),
        ("y", "x", "core", "far", "next", "col"),
    )
    return jax.shard_map(
        body,
        mesh=fine,
        in_specs=(
            P((*REP, *ROW), "col"),
            P((*REP, "col"), ROW),
            P((*REP, "col"), ROW),
            P(ROW, None),
        ),
        out_specs=(P((*REP, "col"), ROW), P(ROW, None)),
        check_vma=False,
    )
```

```python
import functools

import jax
import jax.numpy as jnp
from jax import lax
from jax.experimental import pallas as pl
from jax.experimental.pallas import tpu as pltpu
from jax.sharding import Mesh, PartitionSpec as P

REP = ("y", "x", "core")
NEAR = ("x", "core")
ROW = ("far", "next")
HIGHEST = lax.Precision.HIGHEST


def to_all(block, axes):
    copies = jnp.broadcast_to(block, (lax.axis_size(axes), *block.shape))
    return lax.all_to_all(copies, axes, split_axis=0, concat_axis=0, tiled=True)


def summed_over(block, axes):
    return jnp.sum(to_all(block, axes), axis=0)


def split_and_summed(blocks, axes):
    return jnp.sum(lax.all_to_all(blocks, axes, split_axis=0, concat_axis=0, tiled=True), axis=0)


def shifted(size, by):
    return [(k, (k + by) % size) for k in range(size)]


def dot(a, b, dims, precision=HIGHEST):
    return lax.dot_general(
        a, b, (dims, ((), ())), precision=precision, preferred_element_type=jnp.float32
    )


def thirds(x):
    first = x.astype(jnp.bfloat16)
    rest = x - first.astype(jnp.float32)
    second = rest.astype(jnp.bfloat16)
    third = (rest - second.astype(jnp.float32)).astype(jnp.bfloat16)
    return first, second, third


def mxu(a, b, contract):
    return lax.dot_general(a, b, (contract, ((), ())), preferred_element_type=jnp.float32)


def lanes(ref, start, count):
    return jnp.concatenate([ref[start + k] for k in range(count)], axis=1)


def joined(terms, rank):
    return terms[:rank] + terms[rank : 2 * rank] + terms[2 * rank :]


def projection_kernel(n_col, col_ref, right_ref, grads_ref, sends_ref):
    rank = right_ref.shape[0]
    per = sends_ref.shape[0] // n_col // n_col
    wide = sends_ref.shape[2]
    stack = jnp.concatenate(thirds(right_ref[...]), axis=0)
    proj = joined(mxu(stack, grads_ref[...], ((1,), (1,))), rank)
    for k in range(sends_ref.shape[0]):
        owner = k // n_col
        at = owner % per * wide
        keep = (col_ref[0] == owner // per).astype(jnp.float32)
        sends_ref[k] = proj[:, at : at + wide] * keep


def error_kernel(right_ref, err_ref, out_ref):
    rank = right_ref.shape[0]
    stack = jnp.concatenate(thirds(right_ref[...]), axis=0)
    wide = 256
    for k in range(err_ref.shape[0] // wide):
        high, mid, low = thirds(err_ref[k * wide : (k + 1) * wide])
        terms = joined(mxu(stack, high, ((1,), (1,))) + mxu(stack, mid, ((1,), (1,))), rank)
        out_ref[:, k * wide : (k + 1) * wide] = terms + mxu(stack[:rank], low, ((1,), (1,)))


def left_kernel(mine_ref, acts_ref, part_ref, out_ref):
    rank = mine_ref.shape[1]
    mine = mine_ref[0]
    for k in range(1, mine_ref.shape[0]):
        mine += mine_ref[k]
    stack = jnp.concatenate(thirds(mine), axis=0)
    left = joined(mxu(stack, acts_ref[...], ((1,), (0,))), rank) + part_ref[...]
    wide = out_ref.shape[2]
    for k in range(out_ref.shape[0]):
        out_ref[k] = left[:, k * wide : (k + 1) * wide]


def local_call(kernel, out_shape, *args, scalars=0, limit=16):
    return pl.pallas_call(
        kernel,
        in_specs=[pl.BlockSpec(memory_space=pltpu.SMEM)] * scalars
        + [pl.BlockSpec(memory_space=pltpu.VMEM)] * (len(args) - scalars),
        out_specs=pl.BlockSpec(memory_space=pltpu.VMEM),
        out_shape=jax.ShapeDtypeStruct(out_shape, jnp.float32),
        compiler_params=pltpu.CompilerParams(vmem_limit_bytes=limit * 2**20),
    )(*args)


def target_kernel(replicas, n_pieces, place_ref, *refs):
    pieces, refs = refs[:n_pieces], refs[n_pieces:]
    mine_ref, other_ref, err_ref, left_ref, target_ref, joint_ref, grads = refs
    rank = left_ref.shape[1]
    wide = 256
    depth = pieces[0].shape[0]
    chunk = depth // 2
    same = place_ref[0] == 1
    for k in range(n_pieces):
        source = lax.rem(place_ref[1] + n_pieces - k, n_pieces)
        source = pl.ds(pl.multiple_of(source * chunk, chunk), chunk)
        mine, other = mine_ref[source], other_ref[source]
        grads[k * depth : k * depth + chunk] = jnp.where(same, mine, other)
        grads[k * depth + chunk : (k + 1) * depth] = jnp.where(same, other, mine)
    left = lanes(left_ref, 0, left_ref.shape[0])
    stack = jnp.concatenate(thirds(left), axis=0)
    gram = lax.dot_general(
        left,
        left,
        (((1,), (1,)), ((), ())),
        precision=HIGHEST,
        preferred_element_type=jnp.float32,
    )
    sums = None
    for k in range(err_ref.shape[0] // wide):
        span = slice(k * wide, (k + 1) * wide)
        tile = err_ref[span]
        for n, piece in enumerate(pieces):
            tile += mxu(piece[:, span], grads[n * depth : (n + 1) * depth], ((0,), (0,)))
        target_ref[span] = tile
        high, mid, low = thirds(tile)
        terms = mxu(stack[:, span], high, ((1,), (0,))) + mxu(stack[:, span], mid, ((1,), (0,)))
        right = joined(terms, rank) + mxu(stack[:rank, span], low, ((1,), (0,)))
        sums = right if sums is None else sums + right
    gram = jnp.concatenate([gram, jnp.zeros((rank, 128 - rank), jnp.float32)], axis=1) / replicas
    both = jnp.concatenate([sums, gram], axis=1)
    for k in range(joint_ref.shape[0]):
        first, at = (k % 2) * (rank // 2), (k // 2) * 128
        joint_ref[k] = both[first : first + rank // 2, at : at + 128]


def target_and_terms(pieces, mine, other, err, left, place, replicas):
    rows, cols = err.shape
    rank = left.shape[1]
    tiles = cols // 128 + 1
    in_vmem = pl.BlockSpec(memory_space=pltpu.VMEM)
    return pl.pallas_call(
        functools.partial(target_kernel, replicas, len(pieces)),
        in_specs=[pl.BlockSpec(memory_space=pltpu.SMEM)] + [in_vmem] * (4 + len(pieces)),
        out_specs=[in_vmem, in_vmem],
        out_shape=[
            jax.ShapeDtypeStruct((rows, cols), jnp.float32),
            jax.ShapeDtypeStruct((2 * tiles, rank // 2, 128), jnp.float32),
        ],
        scratch_shapes=[pltpu.VMEM((2 * mine.shape[0], cols), mine.dtype)],
        compiler_params=pltpu.CompilerParams(vmem_limit_bytes=16 * 2**20),
    )(place, *pieces, mine, other, err, left)


def finish_kernel(replicas, joint_ref, left_ref, target_ref, error_ref, right_ref, error, sems):
    rank, cols = right_ref.shape
    halves = [
        jnp.concatenate([joint_ref[2 * c + h] for c in range(joint_ref.shape[0] // 2)], axis=1)
        for h in range(2)
    ]
    joint = jnp.concatenate(halves, axis=0)
    system = jnp.concatenate([joint, lanes(left_ref, 0, left_ref.shape[0])], axis=1)
    row_of = lax.broadcasted_iota(jnp.int32, (rank, 1), 0)
    for k in range(rank - 1):
        column = system[:, cols + k : cols + k + 1]
        factor = jnp.where(row_of > k, column / column[k : k + 1], 0.0)
        system = system - factor * system[k : k + 1]
    square = system[:, cols : cols + 128]
    diagonal = lax.broadcasted_iota(jnp.int32, square.shape, 1) == row_of
    pivots = jnp.sum(jnp.where(diagonal, square, 0.0), axis=1, keepdims=True)
    system = system / jnp.sqrt(pivots)
    right = system[:, :cols] / replicas
    right_ref[...] = right
    first, second, third = thirds(right)
    rights = jnp.concatenate([first, second, first, second, third, first], axis=0)
    first, second, third = thirds(system[:, cols + 128 :])
    orths = jnp.concatenate([first, first, second, second, first, third], axis=0)
    wide = target_ref.shape[0] // sems.shape[0]
    copies = []
    for k in range(sems.shape[0]):
        span = slice(k * wide, (k + 1) * wide)
        error[span] = target_ref[span] - mxu(orths[:, span], rights, ((0,), (0,)))
        copies.append(pltpu.make_async_copy(error.at[span], error_ref.at[span], sems.at[k]))
        copies[-1].start()
    for copy in copies:
        copy.wait()


def finish(joint, left, target, replicas):
    rows, cols = target.shape
    rank = left.shape[1]
    in_vmem = pl.BlockSpec(memory_space=pltpu.VMEM)
    return pl.pallas_call(
        functools.partial(finish_kernel, replicas),
        in_specs=[in_vmem] * 3,
        out_specs=[pl.BlockSpec(memory_space=pl.ANY), in_vmem],
        out_shape=[
            jax.ShapeDtypeStruct((rows, cols), jnp.float32),
            jax.ShapeDtypeStruct((rank, cols), jnp.float32),
        ],
        scratch_shapes=[
            pltpu.VMEM((rows, cols), jnp.float32),
            pltpu.SemaphoreType.DMA((4,)),
        ],
        compiler_params=pltpu.CompilerParams(vmem_limit_bytes=16 * 2**20),
    )(joint, left, target)


def body(acts, grads, err, right):
    rank = right.shape[1]
    rows = err.shape[0]
    n_row, n_col, n_near = lax.axis_size(ROW), lax.axis_size("col"), lax.axis_size(NEAR)
    col = lax.axis_index("col")
    replicas = lax.axis_size(REP)
    n_next = lax.axis_size("next")
    tokens = acts.shape[0]
    right_t = right.T

    with jax.named_scope("gather_inputs"):
        swapped = lax.ppermute(acts, "far", [(0, 1), (1, 0)])
        pair = jnp.concatenate([acts, swapped], axis=0)
        other = lax.ppermute(grads, "col", [(0, 1), (1, 0)])

    with jax.named_scope("left_terms"):
        sends = local_call(
            functools.partial(projection_kernel, n_col),
            (n_row * n_col, rank, tokens),
            col.reshape(1),
            right_t,
            grads,
            scalars=1,
            limit=56,
        )
        mine = lax.all_to_all(sends, (*ROW, "col"), split_axis=0, concat_axis=0, tiled=True)
        part = local_call(error_kernel, (rank, rows), right_t, err)
        blocks = local_call(left_kernel, (n_near, rank, rows // n_near), mine, acts, part)

    with jax.named_scope("left_sum"):
        blocks, pair = lax.optimization_barrier((blocks, pair))
        pieces = [pair, *(lax.ppermute(pair, "next", shifted(n_next, k)) for k in range(1, n_next))]
        part = split_and_summed(blocks, NEAR)
        part = summed_over(part, "y")
        part = summed_over(part, ROW)
        part, other = lax.optimization_barrier((part, other))
        left = to_all(part, NEAR)

    with jax.named_scope("target"):
        target, joint = target_and_terms(
            pieces,
            grads,
            other,
            err,
            left,
            jnp.stack([(col == lax.axis_index("far")).astype(jnp.int32), lax.axis_index("next")]),
            replicas,
        )

    with jax.named_scope("right_sum"):
        part = split_and_summed(joint, NEAR)
        part = summed_over(part, ("y", "col"))
        joint = to_all(part, NEAR)

    with jax.named_scope("finish"):
        new_error, new_right_t = finish(joint, left, target, replicas)
    return new_error, new_right_t.T


def solution(mesh):
    rep, row, col = (mesh.shape[name] for name in ("rep", "row", "col"))
    fine = Mesh(
        mesh.devices.reshape(rep // 8, 4, 2, 2, row // 2, col),
        ("y", "x", "core", "far", "next", "col"),
    )
    return jax.shard_map(
        body,
        mesh=fine,
        in_specs=(
            P((*REP, *ROW), "col"),
            P((*REP, "col"), ROW),
            P((*REP, "col"), ROW),
            P(ROW, None),
        ),
        out_specs=(P((*REP, "col"), ROW), P(ROW, None)),
        check_vma=False,
    )
```

```python
import functools

import jax
import jax.numpy as jnp
from jax import lax
from jax.experimental import pallas as pl
from jax.experimental.pallas import tpu as pltpu
from jax.sharding import Mesh, PartitionSpec as P

REP = ("y", "x", "core")
NEAR = ("x", "core")
ROW = ("far", "next")
HIGHEST = lax.Precision.HIGHEST


def to_all(block, axes):
    copies = jnp.broadcast_to(block, (lax.axis_size(axes), *block.shape))
    return lax.all_to_all(copies, axes, split_axis=0, concat_axis=0, tiled=True)


def summed_over(block, axes):
    return jnp.sum(to_all(block, axes), axis=0)


def split_and_summed(blocks, axes):
    return jnp.sum(lax.all_to_all(blocks, axes, split_axis=0, concat_axis=0, tiled=True), axis=0)


def shifted(size, by):
    return [(k, (k + by) % size) for k in range(size)]


def dot(a, b, dims, precision=HIGHEST):
    return lax.dot_general(
        a, b, (dims, ((), ())), precision=precision, preferred_element_type=jnp.float32
    )


def thirds(x):
    first = x.astype(jnp.bfloat16)
    rest = x - first.astype(jnp.float32)
    second = rest.astype(jnp.bfloat16)
    third = (rest - second.astype(jnp.float32)).astype(jnp.bfloat16)
    return first, second, third


def mxu(a, b, contract):
    return lax.dot_general(a, b, (contract, ((), ())), preferred_element_type=jnp.float32)


def lanes(ref, start, count):
    return jnp.concatenate([ref[start + k] for k in range(count)], axis=1)


def joined(terms, rank):
    return terms[:rank] + terms[rank : 2 * rank] + terms[2 * rank :]


def projection_kernel(n_col, col_ref, right_ref, grads_ref, sends_ref):
    rank = right_ref.shape[0]
    per = sends_ref.shape[0] // n_col // n_col
    wide = sends_ref.shape[2]
    stack = jnp.concatenate(thirds(right_ref[...]), axis=0)
    proj = joined(mxu(stack, grads_ref[...], ((1,), (1,))), rank)
    for k in range(sends_ref.shape[0]):
        owner = k // n_col
        at = owner % per * wide
        keep = (col_ref[0] == owner // per).astype(jnp.float32)
        sends_ref[k] = proj[:, at : at + wide] * keep


def error_kernel(right_ref, err_ref, out_ref):
    rank = right_ref.shape[0]
    stack = jnp.concatenate(thirds(right_ref[...]), axis=0)
    wide = 256
    for k in range(err_ref.shape[0] // wide):
        high, mid, low = thirds(err_ref[k * wide : (k + 1) * wide])
        terms = joined(mxu(stack, high, ((1,), (1,))) + mxu(stack, mid, ((1,), (1,))), rank)
        out_ref[:, k * wide : (k + 1) * wide] = terms + mxu(stack[:rank], low, ((1,), (1,)))


def left_kernel(mine_ref, acts_ref, part_ref, out_ref):
    rank = mine_ref.shape[1]
    mine = mine_ref[0]
    for k in range(1, mine_ref.shape[0]):
        mine += mine_ref[k]
    stack = jnp.concatenate(thirds(mine), axis=0)
    left = joined(mxu(stack, acts_ref[...], ((1,), (0,))), rank) + part_ref[...]
    wide = out_ref.shape[2]
    for k in range(out_ref.shape[0]):
        out_ref[k] = left[:, k * wide : (k + 1) * wide]


def local_call(kernel, out_shape, *args, scalars=0, limit=16):
    return pl.pallas_call(
        kernel,
        in_specs=[pl.BlockSpec(memory_space=pltpu.SMEM)] * scalars
        + [pl.BlockSpec(memory_space=pltpu.VMEM)] * (len(args) - scalars),
        out_specs=pl.BlockSpec(memory_space=pltpu.VMEM),
        out_shape=jax.ShapeDtypeStruct(out_shape, jnp.float32),
        compiler_params=pltpu.CompilerParams(vmem_limit_bytes=limit * 2**20),
    )(*args)


def target_kernel(replicas, n_pieces, place_ref, *refs):
    pieces, refs = refs[:n_pieces], refs[n_pieces:]
    mine_ref, other_ref, err_ref, left_ref, target_ref, joint_ref, grads, target, sems = refs
    rank = left_ref.shape[1]
    wide = 256
    depth = pieces[0].shape[0]
    chunk = depth // 2
    same = place_ref[0] == 1
    for k in range(n_pieces):
        source = lax.rem(place_ref[1] + n_pieces - k, n_pieces)
        source = pl.ds(pl.multiple_of(source * chunk, chunk), chunk)
        mine, other = mine_ref[source], other_ref[source]
        grads[k * depth : k * depth + chunk] = jnp.where(same, mine, other)
        grads[k * depth + chunk : (k + 1) * depth] = jnp.where(same, other, mine)
    left = lanes(left_ref, 0, left_ref.shape[0])
    stack = jnp.concatenate(thirds(left), axis=0)
    gram = lax.dot_general(
        left,
        left,
        (((1,), (1,)), ((), ())),
        precision=HIGHEST,
        preferred_element_type=jnp.float32,
    )
    sums, copies = None, []
    for k in range(err_ref.shape[0] // wide):
        span = slice(k * wide, (k + 1) * wide)
        tile = err_ref[span]
        for n, piece in enumerate(pieces):
            tile += mxu(piece[:, span], grads[n * depth : (n + 1) * depth], ((0,), (0,)))
        target[span] = tile
        copies.append(pltpu.make_async_copy(target.at[span], target_ref.at[span], sems.at[k]))
        copies[-1].start()
        high, mid, low = thirds(tile)
        terms = mxu(stack[:, span], high, ((1,), (0,))) + mxu(stack[:, span], mid, ((1,), (0,)))
        right = joined(terms, rank) + mxu(stack[:rank, span], low, ((1,), (0,)))
        sums = right if sums is None else sums + right
    gram = jnp.concatenate([gram, jnp.zeros((rank, 128 - rank), jnp.float32)], axis=1) / replicas
    both = jnp.concatenate([sums, gram], axis=1)
    for k in range(joint_ref.shape[0]):
        first, at = (k % 2) * (rank // 2), (k // 2) * 128
        joint_ref[k] = both[first : first + rank // 2, at : at + 128]
    for copy in copies:
        copy.wait()


def target_and_terms(pieces, mine, other, err, left, place, replicas):
    rows, cols = err.shape
    rank = left.shape[1]
    tiles = cols // 128 + 1
    in_vmem = pl.BlockSpec(memory_space=pltpu.VMEM)
    return pl.pallas_call(
        functools.partial(target_kernel, replicas, len(pieces)),
        in_specs=[pl.BlockSpec(memory_space=pltpu.SMEM)] + [in_vmem] * (4 + len(pieces)),
        out_specs=[pl.BlockSpec(memory_space=pl.ANY), in_vmem],
        out_shape=[
            jax.ShapeDtypeStruct((rows, cols), jnp.float32),
            jax.ShapeDtypeStruct((2 * tiles, rank // 2, 128), jnp.float32),
        ],
        scratch_shapes=[
            pltpu.VMEM((2 * mine.shape[0], cols), mine.dtype),
            pltpu.VMEM((rows, cols), jnp.float32),
            pltpu.SemaphoreType.DMA((rows // 256,)),
        ],
        compiler_params=pltpu.CompilerParams(vmem_limit_bytes=16 * 2**20),
    )(place, *pieces, mine, other, err, left)


def finish_kernel(
    replicas, joint_ref, left_ref, target_ref, error_ref, right_ref, error, in_sems, sems
):
    rank, cols = right_ref.shape
    wide = error.shape[0] // sems.shape[0]
    spans = [slice(k * wide, (k + 1) * wide) for k in range(sems.shape[0])]
    loads = [
        pltpu.make_async_copy(target_ref.at[span], error.at[span], in_sems.at[k])
        for k, span in enumerate(spans)
    ]
    for load in loads:
        load.start()
    halves = [
        jnp.concatenate([joint_ref[2 * c + h] for c in range(joint_ref.shape[0] // 2)], axis=1)
        for h in range(2)
    ]
    joint = jnp.concatenate(halves, axis=0)
    system = jnp.concatenate([joint, lanes(left_ref, 0, left_ref.shape[0])], axis=1)
    row_of = lax.broadcasted_iota(jnp.int32, (rank, 1), 0)
    for k in range(rank - 1):
        column = system[:, cols + k : cols + k + 1]
        factor = jnp.where(row_of > k, column / column[k : k + 1], 0.0)
        system = system - factor * system[k : k + 1]
    square = system[:, cols : cols + 128]
    diagonal = lax.broadcasted_iota(jnp.int32, square.shape, 1) == row_of
    pivots = jnp.sum(jnp.where(diagonal, square, 0.0), axis=1, keepdims=True)
    system = system / jnp.sqrt(pivots)
    right = system[:, :cols] / replicas
    right_ref[...] = right
    first, second, third = thirds(right)
    rights = jnp.concatenate([first, second, first, second, third, first], axis=0)
    first, second, third = thirds(system[:, cols + 128 :])
    orths = jnp.concatenate([first, first, second, second, first, third], axis=0)
    copies = []
    for k, span in enumerate(spans):
        loads[k].wait()
        error[span] = error[span] - mxu(orths[:, span], rights, ((0,), (0,)))
        copies.append(pltpu.make_async_copy(error.at[span], error_ref.at[span], sems.at[k]))
        copies[-1].start()
    for copy in copies:
        copy.wait()


def finish(joint, left, target, replicas):
    rows, cols = target.shape
    rank = left.shape[1]
    in_vmem = pl.BlockSpec(memory_space=pltpu.VMEM)
    return pl.pallas_call(
        functools.partial(finish_kernel, replicas),
        in_specs=[in_vmem, in_vmem, pl.BlockSpec(memory_space=pl.ANY)],
        out_specs=[pl.BlockSpec(memory_space=pl.ANY), in_vmem],
        out_shape=[
            jax.ShapeDtypeStruct((rows, cols), jnp.float32),
            jax.ShapeDtypeStruct((rank, cols), jnp.float32),
        ],
        scratch_shapes=[
            pltpu.VMEM((rows, cols), jnp.float32),
            pltpu.SemaphoreType.DMA((4,)),
            pltpu.SemaphoreType.DMA((4,)),
        ],
        input_output_aliases={2: 0},
        compiler_params=pltpu.CompilerParams(vmem_limit_bytes=16 * 2**20),
    )(joint, left, target)


def body(acts, grads, err, right):
    rank = right.shape[1]
    rows = err.shape[0]
    n_row, n_col, n_near = lax.axis_size(ROW), lax.axis_size("col"), lax.axis_size(NEAR)
    col = lax.axis_index("col")
    replicas = lax.axis_size(REP)
    n_next = lax.axis_size("next")
    tokens = acts.shape[0]
    right_t = right.T

    with jax.named_scope("gather_inputs"):
        swapped = lax.ppermute(acts, "far", [(0, 1), (1, 0)])
        pair = jnp.concatenate([acts, swapped], axis=0)
        other = lax.ppermute(grads, "col", [(0, 1), (1, 0)])

    with jax.named_scope("left_terms"):
        sends = local_call(
            functools.partial(projection_kernel, n_col),
            (n_row * n_col, rank, tokens),
            col.reshape(1),
            right_t,
            grads,
            scalars=1,
            limit=56,
        )
        mine = lax.all_to_all(sends, (*ROW, "col"), split_axis=0, concat_axis=0, tiled=True)
        part = local_call(error_kernel, (rank, rows), right_t, err)
        blocks = local_call(left_kernel, (n_near, rank, rows // n_near), mine, acts, part)

    with jax.named_scope("left_sum"):
        part = split_and_summed(blocks, NEAR)
        part, pair = lax.optimization_barrier((part, pair))
        pieces = [pair, *(lax.ppermute(pair, "next", shifted(n_next, k)) for k in range(1, n_next))]
        part = summed_over(part, "y")
        part, other = lax.optimization_barrier((part, other))
        part = summed_over(part, ROW)
        left = to_all(part, NEAR)

    with jax.named_scope("target"):
        target, joint = target_and_terms(
            pieces,
            grads,
            other,
            err,
            left,
            jnp.stack([(col == lax.axis_index("far")).astype(jnp.int32), lax.axis_index("next")]),
            replicas,
        )

    with jax.named_scope("right_sum"):
        part = split_and_summed(joint, NEAR)
        part = summed_over(part, ("y", "col"))
        joint = to_all(part, NEAR)

    with jax.named_scope("finish"):
        new_error, new_right_t = finish(joint, left, target, replicas)
    return new_error, new_right_t.T


def solution(mesh):
    rep, row, col = (mesh.shape[name] for name in ("rep", "row", "col"))
    fine = Mesh(
        mesh.devices.reshape(rep // 8, 4, 2, 2, row // 2, col),
        ("y", "x", "core", "far", "next", "col"),
    )
    return jax.shard_map(
        body,
        mesh=fine,
        in_specs=(
            P((*REP, *ROW), "col"),
            P((*REP, "col"), ROW),
            P((*REP, "col"), ROW),
            P(ROW, None),
        ),
        out_specs=(P((*REP, "col"), ROW), P(ROW, None)),
        check_vma=False,
    )
```

```python
import functools

import jax
import jax.numpy as jnp
from jax import lax
from jax.experimental import pallas as pl
from jax.experimental.pallas import tpu as pltpu
from jax.sharding import Mesh, PartitionSpec as P

REP = ("y", "x", "core")
NEAR = ("x", "core")
ROW = ("far", "next")
HIGHEST = lax.Precision.HIGHEST


def to_all(block, axes):
    copies = jnp.broadcast_to(block, (lax.axis_size(axes), *block.shape))
    return lax.all_to_all(copies, axes, split_axis=0, concat_axis=0, tiled=True)


def summed_over(block, axes):
    return jnp.sum(to_all(block, axes), axis=0)


def split_and_summed(blocks, axes):
    return jnp.sum(lax.all_to_all(blocks, axes, split_axis=0, concat_axis=0, tiled=True), axis=0)


def shifted(size, by):
    return [(k, (k + by) % size) for k in range(size)]


def dot(a, b, dims, precision=HIGHEST):
    return lax.dot_general(
        a, b, (dims, ((), ())), precision=precision, preferred_element_type=jnp.float32
    )


def thirds(x):
    first = x.astype(jnp.bfloat16)
    rest = x - first.astype(jnp.float32)
    second = rest.astype(jnp.bfloat16)
    third = (rest - second.astype(jnp.float32)).astype(jnp.bfloat16)
    return first, second, third


def mxu(a, b, contract):
    return lax.dot_general(a, b, (contract, ((), ())), preferred_element_type=jnp.float32)


def lanes(ref, start, count):
    return jnp.concatenate([ref[start + k] for k in range(count)], axis=1)


def joined(terms, rank):
    return terms[:rank] + terms[rank : 2 * rank] + terms[2 * rank :]


def projection_kernel(n_col, col_ref, right_ref, grads_ref, sends_ref):
    rank = right_ref.shape[0]
    per = sends_ref.shape[0] // n_col // n_col
    wide = sends_ref.shape[2]
    stack = jnp.concatenate(thirds(right_ref[...]), axis=0)
    proj = joined(mxu(stack, grads_ref[...], ((1,), (1,))), rank)
    for k in range(sends_ref.shape[0]):
        owner = k // n_col
        at = owner % per * wide
        keep = (col_ref[0] == owner // per).astype(jnp.float32)
        sends_ref[k] = proj[:, at : at + wide] * keep


def error_kernel(right_ref, err_ref, out_ref):
    rank = right_ref.shape[0]
    stack = jnp.concatenate(thirds(right_ref[...]), axis=0)
    wide = 256
    for k in range(err_ref.shape[0] // wide):
        high, mid, low = thirds(err_ref[k * wide : (k + 1) * wide])
        terms = joined(mxu(stack, high, ((1,), (1,))) + mxu(stack, mid, ((1,), (1,))), rank)
        out_ref[:, k * wide : (k + 1) * wide] = terms + mxu(stack[:rank], low, ((1,), (1,)))


def left_kernel(mine_ref, acts_ref, part_ref, out_ref):
    rank = mine_ref.shape[1]
    mine = mine_ref[0]
    for k in range(1, mine_ref.shape[0]):
        mine += mine_ref[k]
    stack = jnp.concatenate(thirds(mine), axis=0)
    left = joined(mxu(stack, acts_ref[...], ((1,), (0,))), rank) + part_ref[...]
    wide = out_ref.shape[2]
    for k in range(out_ref.shape[0]):
        out_ref[k] = left[:, k * wide : (k + 1) * wide]


def local_call(kernel, out_shape, *args, scalars=0, limit=16):
    return pl.pallas_call(
        kernel,
        in_specs=[pl.BlockSpec(memory_space=pltpu.SMEM)] * scalars
        + [pl.BlockSpec(memory_space=pltpu.VMEM)] * (len(args) - scalars),
        out_specs=pl.BlockSpec(memory_space=pltpu.VMEM),
        out_shape=jax.ShapeDtypeStruct(out_shape, jnp.float32),
        compiler_params=pltpu.CompilerParams(vmem_limit_bytes=limit * 2**20),
    )(*args)


def target_kernel(replicas, n_pieces, place_ref, *refs):
    pieces, refs = refs[:n_pieces], refs[n_pieces:]
    mine_ref, other_ref, err_ref, left_ref, target_ref, joint_ref, grads, target, sems = refs
    rank = left_ref.shape[1]
    wide = 256
    depth = pieces[0].shape[0]
    chunk = depth // 2
    same = place_ref[0] == 1
    for k in range(n_pieces):
        source = lax.rem(place_ref[1] + n_pieces - k, n_pieces)
        source = pl.ds(pl.multiple_of(source * chunk, chunk), chunk)
        mine, other = mine_ref[source], other_ref[source]
        grads[k * depth : k * depth + chunk] = jnp.where(same, mine, other)
        grads[k * depth + chunk : (k + 1) * depth] = jnp.where(same, other, mine)
    left = lanes(left_ref, 0, left_ref.shape[0])
    stack = jnp.concatenate(thirds(left), axis=0)
    gram = lax.dot_general(
        left,
        left,
        (((1,), (1,)), ((), ())),
        precision=HIGHEST,
        preferred_element_type=jnp.float32,
    )
    sums, copies = None, []
    for k in range(err_ref.shape[0] // wide):
        span = slice(k * wide, (k + 1) * wide)
        tile = err_ref[span]
        for n, piece in enumerate(pieces):
            tile += mxu(piece[:, span], grads[n * depth : (n + 1) * depth], ((0,), (0,)))
        target[span] = tile
        copies.append(pltpu.make_async_copy(target.at[span], target_ref.at[span], sems.at[k]))
        copies[-1].start()
        high, mid, low = thirds(tile)
        terms = mxu(stack[:, span], high, ((1,), (0,))) + mxu(stack[:, span], mid, ((1,), (0,)))
        right = joined(terms, rank) + mxu(stack[:rank, span], low, ((1,), (0,)))
        sums = right if sums is None else sums + right
    gram = jnp.concatenate([gram, jnp.zeros((rank, 128 - rank), jnp.float32)], axis=1) / replicas
    both = jnp.concatenate([sums, gram], axis=1)
    for k in range(joint_ref.shape[0]):
        first, at = (k % 2) * (rank // 2), (k // 2) * 128
        joint_ref[k] = both[first : first + rank // 2, at : at + 128]
    for copy in copies:
        copy.wait()


def target_and_terms(pieces, mine, other, err, left, place, replicas):
    rows, cols = err.shape
    rank = left.shape[1]
    tiles = cols // 128 + 1
    in_vmem = pl.BlockSpec(memory_space=pltpu.VMEM)
    return pl.pallas_call(
        functools.partial(target_kernel, replicas, len(pieces)),
        in_specs=[pl.BlockSpec(memory_space=pltpu.SMEM)] + [in_vmem] * (4 + len(pieces)),
        out_specs=[pl.BlockSpec(memory_space=pl.ANY), in_vmem],
        out_shape=[
            jax.ShapeDtypeStruct((rows, cols), jnp.float32),
            jax.ShapeDtypeStruct((2 * tiles, rank // 2, 128), jnp.float32),
        ],
        scratch_shapes=[
            pltpu.VMEM((2 * mine.shape[0], cols), mine.dtype),
            pltpu.VMEM((rows, cols), jnp.float32),
            pltpu.SemaphoreType.DMA((rows // 256,)),
        ],
        compiler_params=pltpu.CompilerParams(vmem_limit_bytes=16 * 2**20),
    )(place, *pieces, mine, other, err, left)


def finish_kernel(
    replicas, joint_ref, left_ref, target_ref, error_ref, right_ref, error, in_sems, sems
):
    rank, cols = right_ref.shape
    wide = error.shape[0] // sems.shape[0]
    spans = [slice(k * wide, (k + 1) * wide) for k in range(sems.shape[0])]
    loads = [
        pltpu.make_async_copy(target_ref.at[span], error.at[span], in_sems.at[k])
        for k, span in enumerate(spans)
    ]
    for load in loads:
        load.start()
    halves = [
        jnp.concatenate([joint_ref[2 * c + h] for c in range(joint_ref.shape[0] // 2)], axis=1)
        for h in range(2)
    ]
    joint = jnp.concatenate(halves, axis=0)
    system = jnp.concatenate([joint, lanes(left_ref, 0, left_ref.shape[0])], axis=1)
    row_of = lax.broadcasted_iota(jnp.int32, (rank, 1), 0)
    for k in range(rank - 1):
        column = system[:, cols + k : cols + k + 1]
        factor = jnp.where(row_of > k, column / column[k : k + 1], 0.0)
        system = system - factor * system[k : k + 1]
    square = system[:, cols : cols + 128]
    diagonal = lax.broadcasted_iota(jnp.int32, square.shape, 1) == row_of
    pivots = jnp.sum(jnp.where(diagonal, square, 0.0), axis=1, keepdims=True)
    system = system / jnp.sqrt(pivots)
    right = system[:, :cols] / replicas
    right_ref[...] = right
    first, second, third = thirds(right)
    rights = jnp.concatenate([first, second, first, second, third, first], axis=0)
    first, second, third = thirds(system[:, cols + 128 :])
    orths = jnp.concatenate([first, first, second, second, first, third], axis=0)
    copies = []
    for k, span in enumerate(spans):
        loads[k].wait()
        error[span] = error[span] - mxu(orths[:, span], rights, ((0,), (0,)))
        copies.append(pltpu.make_async_copy(error.at[span], error_ref.at[span], sems.at[k]))
        copies[-1].start()
    for copy in copies:
        copy.wait()


def finish(joint, left, target, replicas):
    rows, cols = target.shape
    rank = left.shape[1]
    in_vmem = pl.BlockSpec(memory_space=pltpu.VMEM)
    return pl.pallas_call(
        functools.partial(finish_kernel, replicas),
        in_specs=[in_vmem, in_vmem, pl.BlockSpec(memory_space=pl.ANY)],
        out_specs=[pl.BlockSpec(memory_space=pl.ANY), in_vmem],
        out_shape=[
            jax.ShapeDtypeStruct((rows, cols), jnp.float32),
            jax.ShapeDtypeStruct((rank, cols), jnp.float32),
        ],
        scratch_shapes=[
            pltpu.VMEM((rows, cols), jnp.float32),
            pltpu.SemaphoreType.DMA((4,)),
            pltpu.SemaphoreType.DMA((4,)),
        ],
        input_output_aliases={2: 0},
        compiler_params=pltpu.CompilerParams(vmem_limit_bytes=16 * 2**20),
    )(joint, left, target)


def body(acts, grads, err, right):
    rank = right.shape[1]
    rows = err.shape[0]
    n_row, n_col, n_near = lax.axis_size(ROW), lax.axis_size("col"), lax.axis_size(NEAR)
    col = lax.axis_index("col")
    replicas = lax.axis_size(REP)
    n_next = lax.axis_size("next")
    tokens = acts.shape[0]
    right_t = right.T

    with jax.named_scope("gather_inputs"):
        swapped = lax.ppermute(acts, "far", [(0, 1), (1, 0)])
        pair = jnp.concatenate([acts, swapped], axis=0)
        other = lax.ppermute(grads, "col", [(0, 1), (1, 0)])

    with jax.named_scope("left_terms"):
        sends = local_call(
            functools.partial(projection_kernel, n_col),
            (n_row * n_col, rank, tokens),
            col.reshape(1),
            right_t,
            grads,
            scalars=1,
            limit=56,
        )
        mine = lax.all_to_all(sends, (*ROW, "col"), split_axis=0, concat_axis=0, tiled=True)
        part = local_call(error_kernel, (rank, rows), right_t, err)
        blocks = local_call(left_kernel, (n_near, rank, rows // n_near), mine, acts, part)

    with jax.named_scope("left_sum"):
        part = split_and_summed(blocks, NEAR)
        part, pair = lax.optimization_barrier((part, pair))
        pieces = [pair, *(lax.ppermute(pair, "next", shifted(n_next, k)) for k in range(1, n_next))]
        part = summed_over(part, "y")
        part = summed_over(part, ROW)
        part, other = lax.optimization_barrier((part, other))
        left = to_all(part, NEAR)

    with jax.named_scope("target"):
        target, joint = target_and_terms(
            pieces,
            grads,
            other,
            err,
            left,
            jnp.stack([(col == lax.axis_index("far")).astype(jnp.int32), lax.axis_index("next")]),
            replicas,
        )

    with jax.named_scope("right_sum"):
        part = split_and_summed(joint, NEAR)
        part = summed_over(part, ("y", "col"))
        joint = to_all(part, NEAR)

    with jax.named_scope("finish"):
        new_error, new_right_t = finish(joint, left, target, replicas)
    return new_error, new_right_t.T


def solution(mesh):
    rep, row, col = (mesh.shape[name] for name in ("rep", "row", "col"))
    fine = Mesh(
        mesh.devices.reshape(rep // 8, 4, 2, 2, row // 2, col),
        ("y", "x", "core", "far", "next", "col"),
    )
    return jax.shard_map(
        body,
        mesh=fine,
        in_specs=(
            P((*REP, *ROW), "col"),
            P((*REP, "col"), ROW),
            P((*REP, "col"), ROW),
            P(ROW, None),
        ),
        out_specs=(P((*REP, "col"), ROW), P(ROW, None)),
        check_vma=False,
    )
```

```python
import functools

import jax
import jax.numpy as jnp
from jax import lax
from jax.experimental import pallas as pl
from jax.experimental.pallas import tpu as pltpu
from jax.sharding import Mesh, PartitionSpec as P

REP = ("y", "x", "core")
NEAR = ("x", "core")
ROW = ("far", "next")
HIGHEST = lax.Precision.HIGHEST


def to_all(block, axes):
    copies = jnp.broadcast_to(block, (lax.axis_size(axes), *block.shape))
    return lax.all_to_all(copies, axes, split_axis=0, concat_axis=0, tiled=True)


def summed_over(block, axes):
    return jnp.sum(to_all(block, axes), axis=0)


def split_and_summed(blocks, axes):
    return jnp.sum(lax.all_to_all(blocks, axes, split_axis=0, concat_axis=0, tiled=True), axis=0)


def shifted(size, by):
    return [(k, (k + by) % size) for k in range(size)]


def dot(a, b, dims, precision=HIGHEST):
    return lax.dot_general(
        a, b, (dims, ((), ())), precision=precision, preferred_element_type=jnp.float32
    )


def thirds(x):
    first = x.astype(jnp.bfloat16)
    rest = x - first.astype(jnp.float32)
    second = rest.astype(jnp.bfloat16)
    third = (rest - second.astype(jnp.float32)).astype(jnp.bfloat16)
    return first, second, third


def mxu(a, b, contract):
    return lax.dot_general(a, b, (contract, ((), ())), preferred_element_type=jnp.float32)


def lanes(ref, start, count):
    return jnp.concatenate([ref[start + k] for k in range(count)], axis=1)


def joined(terms, rank):
    return terms[:rank] + terms[rank : 2 * rank] + terms[2 * rank :]


def projection_kernel(n_col, col_ref, right_ref, grads_ref, sends_ref):
    rank = right_ref.shape[0]
    per = sends_ref.shape[0] // n_col // n_col
    wide = sends_ref.shape[2]
    stack = jnp.concatenate(thirds(right_ref[...]), axis=0)
    proj = joined(mxu(stack, grads_ref[...], ((1,), (1,))), rank)
    for k in range(sends_ref.shape[0]):
        owner = k // n_col
        at = owner % per * wide
        keep = (col_ref[0] == owner // per).astype(jnp.float32)
        sends_ref[k] = proj[:, at : at + wide] * keep


def error_kernel(right_ref, err_ref, out_ref):
    rank = right_ref.shape[0]
    stack = jnp.concatenate(thirds(right_ref[...]), axis=0)
    wide = 256
    for k in range(err_ref.shape[0] // wide):
        high, mid, low = thirds(err_ref[k * wide : (k + 1) * wide])
        terms = joined(mxu(stack, high, ((1,), (1,))) + mxu(stack, mid, ((1,), (1,))), rank)
        out_ref[:, k * wide : (k + 1) * wide] = terms + mxu(stack[:rank], low, ((1,), (1,)))


def left_kernel(mine_ref, acts_ref, part_ref, out_ref):
    rank = mine_ref.shape[1]
    mine = mine_ref[0]
    for k in range(1, mine_ref.shape[0]):
        mine += mine_ref[k]
    stack = jnp.concatenate(thirds(mine), axis=0)
    left = joined(mxu(stack, acts_ref[...], ((1,), (0,))), rank) + part_ref[...]
    wide = out_ref.shape[2]
    for k in range(out_ref.shape[0]):
        out_ref[k] = left[:, k * wide : (k + 1) * wide]


def local_call(kernel, out_shape, *args, scalars=0, limit=16):
    return pl.pallas_call(
        kernel,
        in_specs=[pl.BlockSpec(memory_space=pltpu.SMEM)] * scalars
        + [pl.BlockSpec(memory_space=pltpu.VMEM)] * (len(args) - scalars),
        out_specs=pl.BlockSpec(memory_space=pltpu.VMEM),
        out_shape=jax.ShapeDtypeStruct(out_shape, jnp.float32),
        compiler_params=pltpu.CompilerParams(vmem_limit_bytes=limit * 2**20),
    )(*args)


def target_kernel(n_pieces, place_ref, *refs):
    pieces, refs = refs[:n_pieces], refs[n_pieces:]
    mine_ref, other_ref, err_ref, target_ref, grads, target, sems = refs
    wide = 256
    depth = pieces[0].shape[0]
    chunk = depth // 2
    same = place_ref[0] == 1
    for k in range(n_pieces):
        source = lax.rem(place_ref[1] + n_pieces - k, n_pieces)
        source = pl.ds(pl.multiple_of(source * chunk, chunk), chunk)
        mine, other = mine_ref[source], other_ref[source]
        grads[k * depth : k * depth + chunk] = jnp.where(same, mine, other)
        grads[k * depth + chunk : (k + 1) * depth] = jnp.where(same, other, mine)
    copies = []
    for k in range(err_ref.shape[0] // wide):
        span = slice(k * wide, (k + 1) * wide)
        tile = err_ref[span]
        for n, piece in enumerate(pieces):
            tile += mxu(piece[:, span], grads[n * depth : (n + 1) * depth], ((0,), (0,)))
        target[span] = tile
        copies.append(pltpu.make_async_copy(target.at[span], target_ref.at[span], sems.at[k]))
        copies[-1].start()
    for copy in copies:
        copy.wait()


def target_of(pieces, mine, other, err, place):
    rows, cols = err.shape
    in_vmem = pl.BlockSpec(memory_space=pltpu.VMEM)
    return pl.pallas_call(
        functools.partial(target_kernel, len(pieces)),
        in_specs=[pl.BlockSpec(memory_space=pltpu.SMEM)] + [in_vmem] * (3 + len(pieces)),
        out_specs=pl.BlockSpec(memory_space=pl.ANY),
        out_shape=jax.ShapeDtypeStruct((rows, cols), jnp.float32),
        scratch_shapes=[
            pltpu.VMEM((2 * mine.shape[0], cols), mine.dtype),
            pltpu.VMEM((rows, cols), jnp.float32),
            pltpu.SemaphoreType.DMA((rows // 256,)),
        ],
        compiler_params=pltpu.CompilerParams(vmem_limit_bytes=16 * 2**20),
        cost_estimate=pl.CostEstimate(
            flops=2 * rows * cols * 2 * mine.shape[0], bytes_accessed=8 * rows * cols, transcendentals=0
        ),
    )(place, *pieces, mine, other, err)


def terms_kernel(replicas, left_ref, target_ref, joint_ref, target, sems):
    rank = left_ref.shape[1]
    wide = target.shape[0] // sems.shape[0]
    spans = [slice(k * wide, (k + 1) * wide) for k in range(sems.shape[0])]
    loads = [
        pltpu.make_async_copy(target_ref.at[span], target.at[span], sems.at[k])
        for k, span in enumerate(spans)
    ]
    for load in loads:
        load.start()
    left = lanes(left_ref, 0, left_ref.shape[0])
    stack = jnp.concatenate(thirds(left), axis=0)
    gram = lax.dot_general(
        left,
        left,
        (((1,), (1,)), ((), ())),
        precision=HIGHEST,
        preferred_element_type=jnp.float32,
    )
    right = None
    for load, span in zip(loads, spans):
        load.wait()
        high, mid, low = thirds(target[span])
        terms = mxu(stack[:, span], high, ((1,), (0,))) + mxu(stack[:, span], mid, ((1,), (0,)))
        terms = joined(terms, rank) + mxu(stack[:rank, span], low, ((1,), (0,)))
        right = terms if right is None else right + terms
    gram = jnp.concatenate([gram, jnp.zeros((rank, 128 - rank), jnp.float32)], axis=1) / replicas
    both = jnp.concatenate([right, gram], axis=1)
    for k in range(joint_ref.shape[0]):
        first, at = (k % 2) * (rank // 2), (k // 2) * 128
        joint_ref[k] = both[first : first + rank // 2, at : at + 128]


def terms_of(left, target, replicas):
    rows, cols = target.shape
    rank = left.shape[1]
    in_vmem = pl.BlockSpec(memory_space=pltpu.VMEM)
    return pl.pallas_call(
        functools.partial(terms_kernel, replicas),
        in_specs=[in_vmem, pl.BlockSpec(memory_space=pl.ANY)],
        out_specs=in_vmem,
        out_shape=jax.ShapeDtypeStruct((2 * (cols // 128 + 1), rank // 2, 128), jnp.float32),
        scratch_shapes=[pltpu.VMEM((rows, cols), jnp.float32), pltpu.SemaphoreType.DMA((4,))],
        compiler_params=pltpu.CompilerParams(vmem_limit_bytes=56 * 2**20),
    )(left, target)


def finish_kernel(
    replicas, joint_ref, left_ref, target_ref, error_ref, right_ref, error, in_sems, sems
):
    rank, cols = right_ref.shape
    wide = error.shape[0] // sems.shape[0]
    spans = [slice(k * wide, (k + 1) * wide) for k in range(sems.shape[0])]
    loads = [
        pltpu.make_async_copy(target_ref.at[span], error.at[span], in_sems.at[k])
        for k, span in enumerate(spans)
    ]
    for load in loads:
        load.start()
    halves = [
        jnp.concatenate([joint_ref[2 * c + h] for c in range(joint_ref.shape[0] // 2)], axis=1)
        for h in range(2)
    ]
    joint = jnp.concatenate(halves, axis=0)
    system = jnp.concatenate([joint, lanes(left_ref, 0, left_ref.shape[0])], axis=1)
    row_of = lax.broadcasted_iota(jnp.int32, (rank, 1), 0)
    for k in range(rank - 1):
        column = system[:, cols + k : cols + k + 1]
        factor = jnp.where(row_of > k, column / column[k : k + 1], 0.0)
        system = system - factor * system[k : k + 1]
    square = system[:, cols : cols + 128]
    diagonal = lax.broadcasted_iota(jnp.int32, square.shape, 1) == row_of
    pivots = jnp.sum(jnp.where(diagonal, square, 0.0), axis=1, keepdims=True)
    system = system / jnp.sqrt(pivots)
    right = system[:, :cols] / replicas
    right_ref[...] = right
    first, second, third = thirds(right)
    rights = jnp.concatenate([first, second, first, second, third, first], axis=0)
    first, second, third = thirds(system[:, cols + 128 :])
    orths = jnp.concatenate([first, first, second, second, first, third], axis=0)
    copies = []
    for k, span in enumerate(spans):
        loads[k].wait()
        error[span] = error[span] - mxu(orths[:, span], rights, ((0,), (0,)))
        copies.append(pltpu.make_async_copy(error.at[span], error_ref.at[span], sems.at[k]))
        copies[-1].start()
    for copy in copies:
        copy.wait()


def finish(joint, left, target, replicas):
    rows, cols = target.shape
    rank = left.shape[1]
    in_vmem = pl.BlockSpec(memory_space=pltpu.VMEM)
    return pl.pallas_call(
        functools.partial(finish_kernel, replicas),
        in_specs=[in_vmem, in_vmem, pl.BlockSpec(memory_space=pl.ANY)],
        out_specs=[pl.BlockSpec(memory_space=pl.ANY), in_vmem],
        out_shape=[
            jax.ShapeDtypeStruct((rows, cols), jnp.float32),
            jax.ShapeDtypeStruct((rank, cols), jnp.float32),
        ],
        scratch_shapes=[
            pltpu.VMEM((rows, cols), jnp.float32),
            pltpu.SemaphoreType.DMA((4,)),
            pltpu.SemaphoreType.DMA((4,)),
        ],
        input_output_aliases={2: 0},
        compiler_params=pltpu.CompilerParams(vmem_limit_bytes=16 * 2**20),
    )(joint, left, target)


def body(acts, grads, err, right):
    rank = right.shape[1]
    rows = err.shape[0]
    n_row, n_col, n_near = lax.axis_size(ROW), lax.axis_size("col"), lax.axis_size(NEAR)
    col = lax.axis_index("col")
    replicas = lax.axis_size(REP)
    n_next = lax.axis_size("next")
    tokens = acts.shape[0]
    right_t = right.T

    with jax.named_scope("gather_inputs"):
        swapped = lax.ppermute(acts, "far", [(0, 1), (1, 0)])
        pair = jnp.concatenate([acts, swapped], axis=0)
        other = lax.ppermute(grads, "col", [(0, 1), (1, 0)])

    with jax.named_scope("left_terms"):
        sends = local_call(
            functools.partial(projection_kernel, n_col),
            (n_row * n_col, rank, tokens),
            col.reshape(1),
            right_t,
            grads,
            scalars=1,
            limit=56,
        )
        mine = lax.all_to_all(sends, (*ROW, "col"), split_axis=0, concat_axis=0, tiled=True)
        part = local_call(error_kernel, (rank, rows), right_t, err)
        blocks = local_call(left_kernel, (n_near, rank, rows // n_near), mine, acts, part)

    with jax.named_scope("left_sum"):
        blocks, pair = lax.optimization_barrier((blocks, pair))
        pieces = [pair, *(lax.ppermute(pair, "next", shifted(n_next, k)) for k in range(1, n_next))]
        part = split_and_summed(blocks, NEAR)
        part = summed_over(part, "y")
        part = summed_over(part, ROW)
        part, other = lax.optimization_barrier((part, other))
        left = to_all(part, NEAR)

    with jax.named_scope("target"):
        place = jnp.stack([(col == lax.axis_index("far")).astype(jnp.int32), lax.axis_index("next")])
        target = target_of(pieces, grads, other, err, place)
        joint = terms_of(left, target, replicas)

    with jax.named_scope("right_sum"):
        part = split_and_summed(joint, NEAR)
        part = summed_over(part, ("y", "col"))
        joint = to_all(part, NEAR)

    with jax.named_scope("finish"):
        new_error, new_right_t = finish(joint, left, target, replicas)
    return new_error, new_right_t.T


def solution(mesh):
    rep, row, col = (mesh.shape[name] for name in ("rep", "row", "col"))
    fine = Mesh(
        mesh.devices.reshape(rep // 8, 4, 2, 2, row // 2, col),
        ("y", "x", "core", "far", "next", "col"),
    )
    return jax.shard_map(
        body,
        mesh=fine,
        in_specs=(
            P((*REP, *ROW), "col"),
            P((*REP, "col"), ROW),
            P((*REP, "col"), ROW),
            P(ROW, None),
        ),
        out_specs=(P((*REP, "col"), ROW), P(ROW, None)),
        check_vma=False,
    )
```

```python
import functools

import jax
import jax.numpy as jnp
from jax import lax
from jax.experimental import pallas as pl
from jax.experimental.pallas import tpu as pltpu
from jax.sharding import Mesh, PartitionSpec as P

REP = ("y", "x", "core")
NEAR = ("x", "core")
ROW = ("far", "next")
HIGHEST = lax.Precision.HIGHEST


def to_all(block, axes):
    copies = jnp.broadcast_to(block, (lax.axis_size(axes), *block.shape))
    return lax.all_to_all(copies, axes, split_axis=0, concat_axis=0, tiled=True)


def summed_over(block, axes):
    return jnp.sum(to_all(block, axes), axis=0)


def split_and_summed(blocks, axes):
    return jnp.sum(lax.all_to_all(blocks, axes, split_axis=0, concat_axis=0, tiled=True), axis=0)


def shifted(size, by):
    return [(k, (k + by) % size) for k in range(size)]


def dot(a, b, dims, precision=HIGHEST):
    return lax.dot_general(
        a, b, (dims, ((), ())), precision=precision, preferred_element_type=jnp.float32
    )


def thirds(x):
    first = x.astype(jnp.bfloat16)
    rest = x - first.astype(jnp.float32)
    second = rest.astype(jnp.bfloat16)
    third = (rest - second.astype(jnp.float32)).astype(jnp.bfloat16)
    return first, second, third


def mxu(a, b, contract):
    return lax.dot_general(a, b, (contract, ((), ())), preferred_element_type=jnp.float32)


def lanes(ref, start, count):
    return jnp.concatenate([ref[start + k] for k in range(count)], axis=1)


def joined(terms, rank):
    return terms[:rank] + terms[rank : 2 * rank] + terms[2 * rank :]


def projection_kernel(n_col, col_ref, right_ref, grads_ref, sends_ref):
    rank = right_ref.shape[0]
    per = sends_ref.shape[0] // n_col // n_col
    wide = sends_ref.shape[2]
    stack = jnp.concatenate(thirds(right_ref[...]), axis=0)
    proj = joined(mxu(stack, grads_ref[...], ((1,), (1,))), rank)
    for k in range(sends_ref.shape[0]):
        owner = k // n_col
        at = owner % per * wide
        keep = (col_ref[0] == owner // per).astype(jnp.float32)
        sends_ref[k] = proj[:, at : at + wide] * keep


def error_kernel(right_ref, err_ref, out_ref):
    rank = right_ref.shape[0]
    stack = jnp.concatenate(thirds(right_ref[...]), axis=0)
    wide = 256
    for k in range(err_ref.shape[0] // wide):
        high, mid, low = thirds(err_ref[k * wide : (k + 1) * wide])
        terms = joined(mxu(stack, high, ((1,), (1,))) + mxu(stack, mid, ((1,), (1,))), rank)
        out_ref[:, k * wide : (k + 1) * wide] = terms + mxu(stack[:rank], low, ((1,), (1,)))


def left_kernel(mine_ref, acts_ref, part_ref, out_ref):
    rank = mine_ref.shape[1]
    mine = mine_ref[0]
    for k in range(1, mine_ref.shape[0]):
        mine += mine_ref[k]
    stack = jnp.concatenate(thirds(mine), axis=0)
    left = joined(mxu(stack, acts_ref[...], ((1,), (0,))), rank) + part_ref[...]
    wide = out_ref.shape[2]
    for k in range(out_ref.shape[0]):
        out_ref[k] = left[:, k * wide : (k + 1) * wide]


def local_call(kernel, out_shape, *args, scalars=0, limit=16):
    return pl.pallas_call(
        kernel,
        in_specs=[pl.BlockSpec(memory_space=pltpu.SMEM)] * scalars
        + [pl.BlockSpec(memory_space=pltpu.VMEM)] * (len(args) - scalars),
        out_specs=pl.BlockSpec(memory_space=pltpu.VMEM),
        out_shape=jax.ShapeDtypeStruct(out_shape, jnp.float32),
        compiler_params=pltpu.CompilerParams(vmem_limit_bytes=limit * 2**20),
    )(*args)


def target_kernel(replicas, n_pieces, place_ref, *refs):
    pieces, refs = refs[:n_pieces], refs[n_pieces:]
    mine_ref, other_ref, err_ref, left_ref, target_ref, joint_ref, grads, target, sems = refs
    rank = left_ref.shape[1]
    wide = 256
    depth = pieces[0].shape[0]
    chunk = depth // 2
    same = place_ref[0] == 1
    for k in range(n_pieces):
        source = lax.rem(place_ref[1] + n_pieces - k, n_pieces)
        source = pl.ds(pl.multiple_of(source * chunk, chunk), chunk)
        mine, other = mine_ref[source], other_ref[source]
        grads[k * depth : k * depth + chunk] = jnp.where(same, mine, other)
        grads[k * depth + chunk : (k + 1) * depth] = jnp.where(same, other, mine)
    left = lanes(left_ref, 0, left_ref.shape[0])
    stack = jnp.concatenate(thirds(left), axis=0)
    gram = lax.dot_general(
        left,
        left,
        (((1,), (1,)), ((), ())),
        precision=HIGHEST,
        preferred_element_type=jnp.float32,
    )
    sums, copies = None, []
    for k in range(err_ref.shape[0] // wide):
        span = slice(k * wide, (k + 1) * wide)
        tile = err_ref[span]
        for n, piece in enumerate(pieces):
            tile += mxu(piece[:, span], grads[n * depth : (n + 1) * depth], ((0,), (0,)))
        target[span] = tile
        copies.append(pltpu.make_async_copy(target.at[span], target_ref.at[span], sems.at[k]))
        copies[-1].start()
        high, mid, low = thirds(tile)
        terms = mxu(stack[:, span], high, ((1,), (0,))) + mxu(stack[:, span], mid, ((1,), (0,)))
        right = joined(terms, rank) + mxu(stack[:rank, span], low, ((1,), (0,)))
        sums = right if sums is None else sums + right
    gram = jnp.concatenate([gram, jnp.zeros((rank, 128 - rank), jnp.float32)], axis=1) / replicas
    both = jnp.concatenate([sums, gram], axis=1)
    for k in range(joint_ref.shape[0]):
        first, at = (k % 2) * (rank // 2), (k // 2) * 128
        joint_ref[k] = both[first : first + rank // 2, at : at + 128]
    for copy in copies:
        copy.wait()


def target_and_terms(pieces, mine, other, err, left, place, replicas):
    rows, cols = err.shape
    rank = left.shape[1]
    tiles = cols // 128 + 1
    in_vmem = pl.BlockSpec(memory_space=pltpu.VMEM)
    return pl.pallas_call(
        functools.partial(target_kernel, replicas, len(pieces)),
        in_specs=[pl.BlockSpec(memory_space=pltpu.SMEM)] + [in_vmem] * (4 + len(pieces)),
        out_specs=[pl.BlockSpec(memory_space=pl.ANY), in_vmem],
        out_shape=[
            jax.ShapeDtypeStruct((rows, cols), jnp.float32),
            jax.ShapeDtypeStruct((2 * tiles, rank // 2, 128), jnp.float32),
        ],
        scratch_shapes=[
            pltpu.VMEM((2 * mine.shape[0], cols), mine.dtype),
            pltpu.VMEM((rows, cols), jnp.float32),
            pltpu.SemaphoreType.DMA((rows // 256,)),
        ],
        compiler_params=pltpu.CompilerParams(vmem_limit_bytes=16 * 2**20),
    )(place, *pieces, mine, other, err, left)


def finish_kernel(
    replicas, joint_ref, left_ref, target_ref, error_ref, right_ref, error, in_sems, sems
):
    rank, cols = right_ref.shape
    wide = error.shape[0] // sems.shape[0]
    spans = [slice(k * wide, (k + 1) * wide) for k in range(sems.shape[0])]
    loads = [
        pltpu.make_async_copy(target_ref.at[span], error.at[span], in_sems.at[k])
        for k, span in enumerate(spans)
    ]
    for load in loads:
        load.start()
    halves = [
        jnp.concatenate([joint_ref[2 * c + h] for c in range(joint_ref.shape[0] // 2)], axis=1)
        for h in range(2)
    ]
    joint = jnp.concatenate(halves, axis=0)
    system = jnp.concatenate([joint, lanes(left_ref, 0, left_ref.shape[0])], axis=1)
    row_of = lax.broadcasted_iota(jnp.int32, (rank, 1), 0)
    for k in range(rank - 1):
        column = system[:, cols + k : cols + k + 1]
        factor = jnp.where(row_of > k, column / column[k : k + 1], 0.0)
        system = system - factor * system[k : k + 1]
    square = system[:, cols : cols + 128]
    diagonal = lax.broadcasted_iota(jnp.int32, square.shape, 1) == row_of
    pivots = jnp.sum(jnp.where(diagonal, square, 0.0), axis=1, keepdims=True)
    system = system / jnp.sqrt(pivots)
    right = system[:, :cols] / replicas
    right_ref[...] = right
    first, second, third = thirds(right)
    rights = jnp.concatenate([first, second, first, second, third, first], axis=0)
    first, second, third = thirds(system[:, cols + 128 :])
    orths = jnp.concatenate([first, first, second, second, first, third], axis=0)
    copies = []
    for k, span in enumerate(spans):
        loads[k].wait()
        error[span] = error[span] - mxu(orths[:, span], rights, ((0,), (0,)))
        copies.append(pltpu.make_async_copy(error.at[span], error_ref.at[span], sems.at[k]))
        copies[-1].start()
    for copy in copies:
        copy.wait()


def finish(joint, left, target, replicas):
    rows, cols = target.shape
    rank = left.shape[1]
    in_vmem = pl.BlockSpec(memory_space=pltpu.VMEM)
    return pl.pallas_call(
        functools.partial(finish_kernel, replicas),
        in_specs=[in_vmem, in_vmem, pl.BlockSpec(memory_space=pl.ANY)],
        out_specs=[pl.BlockSpec(memory_space=pl.ANY), in_vmem],
        out_shape=[
            jax.ShapeDtypeStruct((rows, cols), jnp.float32),
            jax.ShapeDtypeStruct((rank, cols), jnp.float32),
        ],
        scratch_shapes=[
            pltpu.VMEM((rows, cols), jnp.float32),
            pltpu.SemaphoreType.DMA((4,)),
            pltpu.SemaphoreType.DMA((4,)),
        ],
        input_output_aliases={2: 0},
        compiler_params=pltpu.CompilerParams(vmem_limit_bytes=16 * 2**20),
    )(joint, left, target)


def body(acts, grads, err, right):
    rank = right.shape[1]
    rows = err.shape[0]
    n_row, n_col, n_near = lax.axis_size(ROW), lax.axis_size("col"), lax.axis_size(NEAR)
    col = lax.axis_index("col")
    replicas = lax.axis_size(REP)
    n_next = lax.axis_size("next")
    tokens = acts.shape[0]
    right_t = right.T

    with jax.named_scope("gather_inputs"):
        other = lax.ppermute(grads, "col", [(0, 1), (1, 0)])

    with jax.named_scope("left_terms"):
        sends = local_call(
            functools.partial(projection_kernel, n_col),
            (n_row * n_col, rank, tokens),
            col.reshape(1),
            right_t,
            grads,
            scalars=1,
            limit=56,
        )
        mine = lax.all_to_all(sends, (*ROW, "col"), split_axis=0, concat_axis=0, tiled=True)
        mine, own = lax.optimization_barrier((mine, acts))
        swapped = lax.ppermute(own, "far", [(0, 1), (1, 0)])
        pair = jnp.concatenate([acts, swapped], axis=0)
        part = local_call(error_kernel, (rank, rows), right_t, err)
        blocks = local_call(left_kernel, (n_near, rank, rows // n_near), mine, acts, part)

    with jax.named_scope("left_sum"):
        part = split_and_summed(blocks, NEAR)
        part, other = lax.optimization_barrier((part, other))
        part = summed_over(part, "y")
        part, pair = lax.optimization_barrier((part, pair))
        pieces = [pair, *(lax.ppermute(pair, "next", shifted(n_next, k)) for k in range(1, n_next))]
        part = summed_over(part, ROW)
        left = to_all(part, NEAR)

    with jax.named_scope("target"):
        target, joint = target_and_terms(
            pieces,
            grads,
            other,
            err,
            left,
            jnp.stack([(col == lax.axis_index("far")).astype(jnp.int32), lax.axis_index("next")]),
            replicas,
        )

    with jax.named_scope("right_sum"):
        part = split_and_summed(joint, NEAR)
        part = summed_over(part, ("y", "col"))
        joint = to_all(part, NEAR)

    with jax.named_scope("finish"):
        new_error, new_right_t = finish(joint, left, target, replicas)
    return new_error, new_right_t.T


def solution(mesh):
    rep, row, col = (mesh.shape[name] for name in ("rep", "row", "col"))
    fine = Mesh(
        mesh.devices.reshape(rep // 8, 4, 2, 2, row // 2, col),
        ("y", "x", "core", "far", "next", "col"),
    )
    return jax.shard_map(
        body,
        mesh=fine,
        in_specs=(
            P((*REP, *ROW), "col"),
            P((*REP, "col"), ROW),
            P((*REP, "col"), ROW),
            P(ROW, None),
        ),
        out_specs=(P((*REP, "col"), ROW), P(ROW, None)),
        check_vma=False,
    )
```

```python
import functools

import jax
import jax.numpy as jnp
from jax import lax
from jax.experimental import pallas as pl
from jax.experimental.pallas import tpu as pltpu
from jax.sharding import Mesh, PartitionSpec as P

REP = ("y", "x", "core")
NEAR = ("x", "core")
ROW = ("far", "next")
HIGHEST = lax.Precision.HIGHEST


def to_all(block, axes):
    copies = jnp.broadcast_to(block, (lax.axis_size(axes), *block.shape))
    return lax.all_to_all(copies, axes, split_axis=0, concat_axis=0, tiled=True)


def summed_over(block, axes):
    return jnp.sum(to_all(block, axes), axis=0)


def split_and_summed(blocks, axes):
    return jnp.sum(lax.all_to_all(blocks, axes, split_axis=0, concat_axis=0, tiled=True), axis=0)


def shifted(size, by):
    return [(k, (k + by) % size) for k in range(size)]


def dot(a, b, dims, precision=HIGHEST):
    return lax.dot_general(
        a, b, (dims, ((), ())), precision=precision, preferred_element_type=jnp.float32
    )


def thirds(x):
    first = x.astype(jnp.bfloat16)
    rest = x - first.astype(jnp.float32)
    second = rest.astype(jnp.bfloat16)
    third = (rest - second.astype(jnp.float32)).astype(jnp.bfloat16)
    return first, second, third


def mxu(a, b, contract):
    return lax.dot_general(a, b, (contract, ((), ())), preferred_element_type=jnp.float32)


def lanes(ref, start, count):
    return jnp.concatenate([ref[start + k] for k in range(count)], axis=1)


def joined(terms, rank):
    return terms[:rank] + terms[rank : 2 * rank] + terms[2 * rank :]


def projection_kernel(n_col, col_ref, right_ref, grads_ref, sends_ref):
    rank = right_ref.shape[0]
    per = sends_ref.shape[0] // n_col // n_col
    wide = sends_ref.shape[2]
    stack = jnp.concatenate(thirds(right_ref[...]), axis=0)
    proj = joined(mxu(stack, grads_ref[...], ((1,), (1,))), rank)
    for k in range(sends_ref.shape[0]):
        owner = k // n_col
        at = owner % per * wide
        keep = (col_ref[0] == owner // per).astype(jnp.float32)
        sends_ref[k] = proj[:, at : at + wide] * keep


def error_kernel(right_ref, err_ref, out_ref):
    rank = right_ref.shape[0]
    stack = jnp.concatenate(thirds(right_ref[...]), axis=0)
    wide = 256
    for k in range(err_ref.shape[0] // wide):
        high, mid, low = thirds(err_ref[k * wide : (k + 1) * wide])
        terms = joined(mxu(stack, high, ((1,), (1,))) + mxu(stack, mid, ((1,), (1,))), rank)
        out_ref[:, k * wide : (k + 1) * wide] = terms + mxu(stack[:rank], low, ((1,), (1,)))


def left_kernel(mine_ref, acts_ref, part_ref, out_ref):
    rank = mine_ref.shape[1]
    mine = mine_ref[0]
    for k in range(1, mine_ref.shape[0]):
        mine += mine_ref[k]
    stack = jnp.concatenate(thirds(mine), axis=0)
    left = joined(mxu(stack, acts_ref[...], ((1,), (0,))), rank) + part_ref[...]
    wide = out_ref.shape[2]
    for k in range(out_ref.shape[0]):
        out_ref[k] = left[:, k * wide : (k + 1) * wide]


def local_call(kernel, out_shape, *args, scalars=0, limit=16):
    return pl.pallas_call(
        kernel,
        in_specs=[pl.BlockSpec(memory_space=pltpu.SMEM)] * scalars
        + [pl.BlockSpec(memory_space=pltpu.VMEM)] * (len(args) - scalars),
        out_specs=pl.BlockSpec(memory_space=pltpu.VMEM),
        out_shape=jax.ShapeDtypeStruct(out_shape, jnp.float32),
        compiler_params=pltpu.CompilerParams(vmem_limit_bytes=limit * 2**20),
    )(*args)


def target_kernel(replicas, n_pieces, place_ref, *refs):
    pieces, refs = refs[:n_pieces], refs[n_pieces:]
    mine_ref, other_ref, err_ref, left_ref, target_ref, joint_ref, grads, target, sems = refs
    rank = left_ref.shape[1]
    wide = 256
    depth = pieces[0].shape[0]
    chunk = depth // 2
    same = place_ref[0] == 1
    for k in range(n_pieces):
        source = lax.rem(place_ref[1] + n_pieces - k, n_pieces)
        source = pl.ds(pl.multiple_of(source * chunk, chunk), chunk)
        mine, other = mine_ref[source], other_ref[source]
        grads[k * depth : k * depth + chunk] = jnp.where(same, mine, other)
        grads[k * depth + chunk : (k + 1) * depth] = jnp.where(same, other, mine)
    left = lanes(left_ref, 0, left_ref.shape[0])
    stack = jnp.concatenate(thirds(left), axis=0)
    gram = lax.dot_general(
        left,
        left,
        (((1,), (1,)), ((), ())),
        precision=HIGHEST,
        preferred_element_type=jnp.float32,
    )
    sums, copies = None, []
    for k in range(err_ref.shape[0] // wide):
        span = slice(k * wide, (k + 1) * wide)
        tile = err_ref[span]
        for n, piece in enumerate(pieces):
            tile += mxu(piece[:, span], grads[n * depth : (n + 1) * depth], ((0,), (0,)))
        target[span] = tile
        copies.append(pltpu.make_async_copy(target.at[span], target_ref.at[span], sems.at[k]))
        copies[-1].start()
        high, mid, low = thirds(tile)
        terms = mxu(stack[:, span], high, ((1,), (0,))) + mxu(stack[:, span], mid, ((1,), (0,)))
        right = joined(terms, rank) + mxu(stack[:rank, span], low, ((1,), (0,)))
        sums = right if sums is None else sums + right
    gram = jnp.concatenate([gram, jnp.zeros((rank, 128 - rank), jnp.float32)], axis=1) / replicas
    both = jnp.concatenate([sums, gram], axis=1)
    for k in range(joint_ref.shape[0]):
        first, at = (k % 2) * (rank // 2), (k // 2) * 128
        joint_ref[k] = both[first : first + rank // 2, at : at + 128]
    for copy in copies:
        copy.wait()


def target_and_terms(pieces, mine, other, err, left, place, replicas):
    rows, cols = err.shape
    rank = left.shape[1]
    tiles = cols // 128 + 1
    in_vmem = pl.BlockSpec(memory_space=pltpu.VMEM)
    return pl.pallas_call(
        functools.partial(target_kernel, replicas, len(pieces)),
        in_specs=[pl.BlockSpec(memory_space=pltpu.SMEM)] + [in_vmem] * (4 + len(pieces)),
        out_specs=[pl.BlockSpec(memory_space=pl.ANY), in_vmem],
        out_shape=[
            jax.ShapeDtypeStruct((rows, cols), jnp.float32),
            jax.ShapeDtypeStruct((2 * tiles, rank // 2, 128), jnp.float32),
        ],
        scratch_shapes=[
            pltpu.VMEM((2 * mine.shape[0], cols), mine.dtype),
            pltpu.VMEM((rows, cols), jnp.float32),
            pltpu.SemaphoreType.DMA((rows // 256,)),
        ],
        compiler_params=pltpu.CompilerParams(vmem_limit_bytes=16 * 2**20),
    )(place, *pieces, mine, other, err, left)


def finish_kernel(
    replicas, joint_ref, left_ref, target_ref, error_ref, right_ref, error, in_sems, sems
):
    rank, cols = right_ref.shape
    wide = error.shape[0] // sems.shape[0]
    spans = [slice(k * wide, (k + 1) * wide) for k in range(sems.shape[0])]
    loads = [
        pltpu.make_async_copy(target_ref.at[span], error.at[span], in_sems.at[k])
        for k, span in enumerate(spans)
    ]
    for load in loads:
        load.start()
    halves = [
        jnp.concatenate([joint_ref[2 * c + h] for c in range(joint_ref.shape[0] // 2)], axis=1)
        for h in range(2)
    ]
    joint = jnp.concatenate(halves, axis=0)
    system = jnp.concatenate([joint, lanes(left_ref, 0, left_ref.shape[0])], axis=1)
    row_of = lax.broadcasted_iota(jnp.int32, (rank, 1), 0)
    for k in range(rank - 1):
        column = system[:, cols + k : cols + k + 1]
        factor = jnp.where(row_of > k, column / column[k : k + 1], 0.0)
        system = system - factor * system[k : k + 1]
    square = system[:, cols : cols + 128]
    diagonal = lax.broadcasted_iota(jnp.int32, square.shape, 1) == row_of
    pivots = jnp.sum(jnp.where(diagonal, square, 0.0), axis=1, keepdims=True)
    system = system / jnp.sqrt(pivots)
    right = system[:, :cols] / replicas
    right_ref[...] = right
    first, second, third = thirds(right)
    rights = jnp.concatenate([first, second, first, second, third, first], axis=0)
    first, second, third = thirds(system[:, cols + 128 :])
    orths = jnp.concatenate([first, first, second, second, first, third], axis=0)
    copies = []
    for k, span in enumerate(spans):
        loads[k].wait()
        error[span] = error[span] - mxu(orths[:, span], rights, ((0,), (0,)))
        copies.append(pltpu.make_async_copy(error.at[span], error_ref.at[span], sems.at[k]))
        copies[-1].start()
    for copy in copies:
        copy.wait()


def finish(joint, left, target, replicas):
    rows, cols = target.shape
    rank = left.shape[1]
    in_vmem = pl.BlockSpec(memory_space=pltpu.VMEM)
    return pl.pallas_call(
        functools.partial(finish_kernel, replicas),
        in_specs=[in_vmem, in_vmem, pl.BlockSpec(memory_space=pl.ANY)],
        out_specs=[pl.BlockSpec(memory_space=pl.ANY), in_vmem],
        out_shape=[
            jax.ShapeDtypeStruct((rows, cols), jnp.float32),
            jax.ShapeDtypeStruct((rank, cols), jnp.float32),
        ],
        scratch_shapes=[
            pltpu.VMEM((rows, cols), jnp.float32),
            pltpu.SemaphoreType.DMA((4,)),
            pltpu.SemaphoreType.DMA((4,)),
        ],
        input_output_aliases={2: 0},
        compiler_params=pltpu.CompilerParams(vmem_limit_bytes=16 * 2**20),
    )(joint, left, target)


def body(acts, grads, err, right):
    rank = right.shape[1]
    rows = err.shape[0]
    n_row, n_col, n_near = lax.axis_size(ROW), lax.axis_size("col"), lax.axis_size(NEAR)
    col = lax.axis_index("col")
    replicas = lax.axis_size(REP)
    n_next = lax.axis_size("next")
    tokens = acts.shape[0]
    right_t = right.T

    with jax.named_scope("gather_inputs"):
        swapped = lax.ppermute(acts, "far", [(0, 1), (1, 0)])
        pair = jnp.concatenate([acts, swapped], axis=0)
        other = lax.ppermute(grads, "col", [(0, 1), (1, 0)])

    with jax.named_scope("left_terms"):
        sends = local_call(
            functools.partial(projection_kernel, n_col),
            (n_row * n_col, rank, tokens),
            col.reshape(1),
            right_t,
            grads,
            scalars=1,
            limit=56,
        )
        mine = lax.all_to_all(sends, (*ROW, "col"), split_axis=0, concat_axis=0, tiled=True)
        part = local_call(error_kernel, (rank, rows), right_t, err)
        blocks = local_call(left_kernel, (n_near, rank, rows // n_near), mine, acts, part)

    with jax.named_scope("left_sum"):
        blocks, pair = lax.optimization_barrier((blocks, pair))
        pieces = [pair, *(lax.ppermute(pair, "next", shifted(n_next, k)) for k in range(1, n_next))]
        part = split_and_summed(blocks, NEAR)
        part = summed_over(part, "y")
        part = summed_over(part, ROW)
        part, other = lax.optimization_barrier((part, other))
        left = to_all(part, NEAR)

    with jax.named_scope("target"):
        target, joint = target_and_terms(
            pieces,
            grads,
            other,
            err,
            left,
            jnp.stack([(col == lax.axis_index("far")).astype(jnp.int32), lax.axis_index("next")]),
            replicas,
        )

    with jax.named_scope("right_sum"):
        part = split_and_summed(joint, NEAR)
        part = summed_over(part, ("y", "col"))
        joint = to_all(part, NEAR)

    with jax.named_scope("finish"):
        new_error, new_right_t = finish(joint, left, target, replicas)
    return new_error, new_right_t.T


def solution(mesh):
    rep, row, col = (mesh.shape[name] for name in ("rep", "row", "col"))
    fine = Mesh(
        mesh.devices.reshape(rep // 8, 4, 2, 2, row // 2, col),
        ("y", "x", "core", "far", "next", "col"),
    )
    return jax.shard_map(
        body,
        mesh=fine,
        in_specs=(
            P((*REP, *ROW), "col"),
            P((*REP, "col"), ROW),
            P((*REP, "col"), ROW),
            P(ROW, None),
        ),
        out_specs=(P((*REP, "col"), ROW), P(ROW, None)),
        check_vma=False,
    )
```
